32 devices in a mesh: node: 8 (over y, x, core), col: 4 (over z).
Axes of the slice: x: 2, y: 2, z: 4, core: 2. Of those that a mesh axis runs over, the one named last changes fastest.
Arguments:
- features: float32 [128, 8192], P('col', 'node'), may hold values from -6 to 6
- tiles: float32 [64, 64, 128, 128], P('node'), may hold values from -0.0625 to 0.0625
- tile_column: int32 [64, 64], P('node'), may hold values from 0 to 63, as said below
- tile_count: int32 [64], P('node'), may hold values from 1 to 64
- labels: int32 [8192], P('node'), may hold values from 0 to 171
- train_mask: int32 [8192], P('node'), may hold values from 0 to 1
- weight_in: float32 [128, 256], P('col'), may hold values from -0.5 to 0.5
- bias_in: float32 [256], P('col'), may hold values from -3 to 3
- weight_out: float32 [256, 172], P('col'), may hold values from -0.75 to 0.75
- bias_out: float32 [172], replicated, may hold values from -4 to 304
Outputs:
- logits: float32 [172, 8192], P(None, 'node')
- mean_loss: float32 [], replicated
- grad_weight_in: float32 [128, 256], P('col')
- grad_bias_in: float32 [256], P('col')
- grad_weight_out: float32 [256, 172], P('col')
- grad_bias_out: float32 [172], replicated
The draws below stay inside these ranges and needn't reach their ends.
Inputs may be any that keep to these rules, and one draw needn't show every extreme that they name: `tile_column`: slot 0 of block row r names block column r; live slots mostly name block columns of the same 1024 nodes or of nearby ones, a few name any block column.
All inputs are finite; a program needn't handle non-finite values.
Results may differ from the reference program's by a relative error of at most 0.0003.
Values sent between devices are 32-bit elements; how exact they have to be, the bound alone decides.
No kernel may reach another device: no remote copies, remote signals or barrier semaphores. Data moves between devices by JAX's collectives and lax.ppermute only.
A program may use at most 128 MiB of HBM per device.

```python
import jax
import jax.numpy as jnp
from jax import lax

FEAT = 128
UNITS = 256
CLASSES = 172
BLOCK = 128
SLOTS = 64
BLOCKS_DEV = 8
NODES = 8192
BLOCKS = 64


def draw_tile_column(key, part):
    key = jax.random.fold_in(key, 11)
    first, second, third, fourth = jax.random.split(key, 4)
    groups = BLOCKS // BLOCKS_DEV
    row_ids = jnp.arange(BLOCKS, dtype=jnp.int32)[:, None]
    owner = row_ids // BLOCKS_DEV
    kind = jax.random.randint(first, (BLOCKS, SLOTS), 0, 4)
    nearby = jax.random.randint(second, (BLOCKS, SLOTS), -2, 3)
    faraway = jax.random.randint(third, (BLOCKS, SLOTS), 0, groups)
    offset = jnp.where(kind < 2, 0, jnp.where(kind == 2, nearby, faraway))
    inside = jax.random.randint(fourth, (BLOCKS, SLOTS), 0, BLOCKS_DEV)
    target = (owner + offset) % groups * BLOCKS_DEV + inside
    slot_ids = jnp.arange(SLOTS, dtype=jnp.int32)[None, :]
    return jnp.where(slot_ids == 0, row_ids, target).astype(jnp.int32)


def draw_tile_count(key, part):
    key = jax.random.fold_in(key, 12)
    first, second = jax.random.split(key)
    groups = BLOCKS // BLOCKS_DEV
    level = jax.random.randint(first, (groups,), SLOTS // 2, SLOTS + 1)
    counts = jax.random.randint(second, (BLOCKS,), 1, SLOTS + 1)
    row_ids = jnp.arange(BLOCKS, dtype=jnp.int32)
    counts = jnp.minimum(counts, level[row_ids // BLOCKS_DEV])
    return jnp.where(row_ids == 0, SLOTS, counts).astype(jnp.int32)


def draw_train_mask(key, part):
    key = jax.random.fold_in(key, 13)
    position = jnp.arange(NODES, dtype=jnp.int32)
    threshold = 250 + 500 * position // NODES
    sample = jax.random.randint(key, (NODES,), 0, 1000)
    return (sample < threshold).astype(jnp.int32)


def draw_bias_out(key, part):
    key = jax.random.fold_in(key, 14)
    first = jax.random.fold_in(key, 0)
    base = jnp.clip(jax.random.normal(first, (CLASSES,), jnp.float32), -4.0, 4.0)
    return base


def with_ends(values, rng, least, high):
    longest = values.shape.index(max(values.shape))
    spots = []
    for shift in (0, 1):
        where = [jax.random.randint(jax.random.fold_in(rng, axis), (), 0, length) for axis, length in enumerate(values.shape)]
        where[longest] = (where[longest] + shift) % values.shape[longest]
        spots.append(tuple(where))
    return values.at[spots[0]].set(least).at[spots[1]].set(high)


def levels(stream_key, dims, cuts, low, top_value):
    def one(axis_at, parts):
        steps = jax.random.uniform(jax.random.fold_in(jax.random.fold_in(stream_key, 6), axis_at), (parts,), jnp.float32, low / len(cuts), top_value / len(cuts))
        return jnp.repeat(jnp.exp(steps), dims[axis_at] // parts).reshape((-1,) + (1,) * (len(dims) - axis_at - 1))

    loudness = one(*cuts[0])
    for cut in cuts[1:]:
        loudness = loudness * one(*cut)
    return loudness


def gaussian(stream_key, shape, width, limit, pieces=(), kind=jnp.bfloat16):
    gain = levels(stream_key, shape, pieces, -0.22, 0.18) if pieces else 1.0
    drawn = jax.random.normal(stream_key, shape, jnp.float32) * width * gain
    return jnp.minimum(jnp.maximum(drawn, -limit), limit).astype(kind)


def setup_inputs(seed: int = 0) -> dict:
    arg_keys = jax.random.split(jax.random.key(seed), 11)
    features = gaussian(arg_keys[0], (FEAT, NODES), 1.0, 6.0, ((0, 4), (1, 8)), jnp.float32)
    tiles = gaussian(arg_keys[1], (BLOCKS, SLOTS, BLOCK, BLOCK), (SLOTS * BLOCK) ** -0.5, 0.0625, ((0, 8),), jnp.float32)
    tile_column = draw_tile_column(jax.random.fold_in(arg_keys[10], 71), 0)
    tile_count = draw_tile_count(jax.random.fold_in(arg_keys[10], 71), 0)
    labels = with_ends(jax.random.randint(arg_keys[4], (NODES,), 0, CLASSES), jax.random.fold_in(arg_keys[4], 1), 0, CLASSES - 1).astype(jnp.int32)
    train_mask = draw_train_mask(jax.random.fold_in(arg_keys[10], 71), 0)
    weight_in = gaussian(arg_keys[6], (FEAT, UNITS), FEAT ** -0.5, 0.5, ((0, 4),), jnp.float32)
    bias_in = gaussian(arg_keys[7], (UNITS,), 0.5, 3.0, ((0, 4),), jnp.float32)
    weight_out = gaussian(arg_keys[8], (UNITS, CLASSES), (UNITS // 4) ** -0.5, 0.75, ((0, 4),), jnp.float32)
    bias_out = draw_bias_out(jax.random.fold_in(arg_keys[10], 71), 0)
    return {"features": features, "tiles": tiles, "tile_column": tile_column, "tile_count": tile_count, "labels": labels, "train_mask": train_mask, "weight_in": weight_in, "bias_in": bias_in, "weight_out": weight_out, "bias_out": bias_out}


precise = lax.Precision.HIGHEST

def aggregate(values, tiles, tile_column, live_slots):
    channel_count = values.shape[0]
    block_view = values.reshape(channel_count, -1, BLOCK)

    def row_block(inputs):
        tile_set, columns, alive = inputs
        picked = block_view[:, columns] * alive[None, :, None]
        return jnp.einsum('fkj,kij->fi', picked, tile_set, precision=precise)
    stacked = lax.map(row_block, (tiles, tile_column, live_slots))
    return jnp.transpose(stacked, (1, 0, 2)).reshape(channel_count, -1)

def reference(features, tiles, tile_column, tile_count, labels, train_mask, weight_in, bias_in, weight_out, bias_out):
    live_slots = (jnp.arange(SLOTS, dtype=jnp.int32)[None, :] < tile_count[:, None]).astype(jnp.float32)
    train_weight = train_mask.astype(jnp.float32)
    label_table = (jnp.arange(CLASSES, dtype=jnp.int32)[:, None] == labels[None, :]).astype(jnp.float32)
    mixed_in = aggregate(features, tiles, tile_column, live_slots)

    def objective(weight_first, bias_first, weight_second, bias_second):
        inner_act = jnp.dot(weight_first.T, mixed_in, precision=precise) + bias_first[:, None]
        hidden = jax.nn.gelu(inner_act, approximate=True)
        mixed_out = aggregate(hidden, tiles, tile_column, live_slots)
        scores = jnp.dot(weight_second.T, mixed_out, precision=precise) + bias_second[:, None]
        log_total = jax.nn.logsumexp(scores, axis=0)
        cross_entropy = log_total - lax.optimization_barrier(jnp.sum(label_table * scores, axis=0))
        return (jnp.sum(train_weight * cross_entropy), scores)
    (loss_total, logits), grads = jax.value_and_grad(objective, argnums=(0, 1, 2, 3), has_aux=True)(weight_in, bias_in, weight_out, bias_out)
    mean_loss = loss_total / jnp.maximum(jnp.sum(train_weight), 1.0)
    return (logits, mean_loss, grads[0], grads[1], grads[2], grads[3])
```

```python
import functools

import jax
import jax.numpy as jnp
from jax import lax
from jax.experimental import pallas as pl
from jax.experimental.pallas import tpu as pltpu
from jax.sharding import PartitionSpec as P

BLOCK = 128
CHUNK = 4
UNROLL = 2
FETCH = 4
PAD = 48

f32 = jnp.float32
bf16 = jnp.bfloat16
VMEM = pl.BlockSpec(memory_space=pltpu.VMEM)
SMEM = pl.BlockSpec(memory_space=pltpu.SMEM)
MIB = 1 << 20

CURVE = 0.7978845608028654
CUBIC = 0.044715


def exchange(value, axis, offset):
    total = lax.axis_size(axis)
    return lax.ppermute(value, axis, [(i, i ^ offset) for i in range(total)])


def split(value):
    high = value.astype(bf16)
    low = (value - high.astype(f32)).astype(bf16)
    return high, low


def product(left, right, dims):
    lh, ll = split(left)
    rh, rl = split(right)

    def one(a, b):
        return lax.dot_general(a, b, (dims, ((), ())), preferred_element_type=f32)

    return one(lh, rh) + (one(lh, rl) + one(ll, rh))


def call(body, outs, scratch, *args, specs=None, out_specs=None, limit=12, flops=0, moved=0):
    return pl.pallas_call(
        body,
        out_shape=outs,
        in_specs=specs or [VMEM] * len(args),
        out_specs=out_specs or [VMEM] * len(outs),
        scratch_shapes=scratch,
        compiler_params=pltpu.CompilerParams(vmem_limit_bytes=limit * MIB),
        cost_estimate=pl.CostEstimate(flops=flops, bytes_accessed=moved, transcendentals=0),
    )(*args)


def pack_body(count_ref, column_ref, tiles_ref, pack_ref, list_ref, row_ref, total_ref, land, store, place, owner, sem, out_sem):
    rows, slots = column_ref.shape

    def copies(row, act):
        buffer = lax.rem(row, 2)

        def one(group, _):
            part = pl.ds(group * FETCH, FETCH)
            copy = pltpu.make_async_copy(
                tiles_ref.at[row, part], land.at[buffer, part], sem.at[buffer, group]
            )
            act(copy)
            return 0

        lax.fori_loop(0, (count_ref[row] + FETCH - 1) // FETCH, one, 0)

    def leave(item):
        return pltpu.make_async_copy(store.at[item], pack_ref.at[item], out_sem.at[item])

    def start(copy):
        copy.start()

    def wait(copy):
        copy.wait()

    def blank_item(item):
        for q in range(CHUNK):
            list_ref[item * CHUNK + q] = 0

    copies(0, start)

    def one_row(row, begin):
        buffer = lax.rem(row, 2)
        live = count_ref[row]

        @pl.when(row + 1 < rows)
        def _():
            copies(row + 1, start)

        def clear(slot, _):
            place[column_ref[row, slot]] = -1
            return 0

        lax.fori_loop(0, live, clear, 0)
        copies(row, wait)

        def scan(slot, found):
            column = column_ref[row, slot]
            at = place[column]
            fresh = at < 0

            @pl.when(fresh)
            def _():
                place[column] = slot
                owner[found] = slot
                list_ref[begin * CHUNK + found] = column

            @pl.when(jnp.logical_not(fresh))
            def _():
                land[buffer, at] = land[buffer, at] + land[buffer, slot]

            return found + fresh.astype(jnp.int32)

        found = lax.fori_loop(0, live, scan, 0)
        steps = (found + CHUNK - 1) // CHUNK

        def blank(index, _):
            list_ref[begin * CHUNK + index] = 0
            return 0

        lax.fori_loop(found, steps * CHUNK, blank, 0)

        def convert(step, _):
            item = begin + step
            row_ref[item] = row
            for q in range(CHUNK):
                index = step * CHUNK + q
                at = slice(q * BLOCK, (q + 1) * BLOCK)

                @pl.when(index < found)
                def _():
                    high, low = split(land[buffer, owner[index]])
                    store[item, :BLOCK, at] = high
                    store[item, BLOCK:, at] = low

                @pl.when(index >= found)
                def _():
                    store[item, :, at] = jnp.zeros((2 * BLOCK, BLOCK), bf16)

            leave(item).start()
            return 0

        lax.fori_loop(0, steps, convert, 0)
        return begin + steps

    used = lax.fori_loop(0, rows, one_row, 0)
    total = (used + UNROLL - 1) // UNROLL * UNROLL

    def fill(item, _):
        row_ref[item] = 0
        blank_item(item)
        store[item] = jnp.zeros(store.shape[1:], bf16)
        leave(item).start()
        return 0

    lax.fori_loop(used, total, fill, 0)
    total_ref[0] = total // UNROLL

    def last(item, _):
        leave(item).wait()
        return 0

    lax.fori_loop(0, total, last, 0)


def pack(tiles, tile_column, tile_count, block_total):
    rows, slots = tile_column.shape
    items = -(-rows * slots // (CHUNK * UNROLL)) * UNROLL
    shape = jax.ShapeDtypeStruct
    return call(
        pack_body,
        [
            pltpu.HBM((items, 2 * BLOCK, CHUNK * BLOCK), bf16),
            shape((items * CHUNK,), jnp.int32),
            shape((items,), jnp.int32),
            shape((1,), jnp.int32),
        ],
        [
            pltpu.VMEM((2, slots, BLOCK, BLOCK), f32),
            pltpu.VMEM((items, 2 * BLOCK, CHUNK * BLOCK), bf16),
            pltpu.SMEM((block_total,), jnp.int32),
            pltpu.SMEM((slots,), jnp.int32),
            pltpu.SemaphoreType.DMA((2, slots // FETCH)),
            pltpu.SemaphoreType.DMA((items,)),
        ],
        tile_count,
        tile_column,
        tiles,
        specs=[SMEM, SMEM, pl.BlockSpec(memory_space=pl.ANY)],
        out_specs=[pl.BlockSpec(memory_space=pltpu.HBM), SMEM, SMEM, SMEM],
        limit=48,
        flops=10**8,
        moved=40 * MIB,
    )


def bring(total_ref, pack_ref, store, sem):
    def one(group):
        part = pl.ds(group * UNROLL, UNROLL)
        return pltpu.make_async_copy(pack_ref.at[part], store.at[part], sem.at[group])

    def start(group, _):
        one(group).start()
        return 0

    lax.fori_loop(0, total_ref[0], start, 0)
    return one


def store_block(values, at, value):
    channels = value.shape[0]
    high, low = split(value)
    values[at, :channels] = high
    values[at, channels:] = low


def mix_rows(total_ref, list_ref, row_ref, one, store, values, sums):
    sums[...] = jnp.zeros_like(sums)

    def step(group, _):
        one(group).wait()
        for part in range(UNROLL):
            item = group * UNROLL + part
            left = jnp.concatenate([values[list_ref[item * CHUNK + q]] for q in range(CHUNK)], axis=1)
            row = row_ref[item]
            sums[row] = sums[row] + lax.dot_general(
                left, store[item], (((1,), (1,)), ((), ())), preferred_element_type=f32
            )
        return 0

    lax.fori_loop(0, total_ref[0], step, 0)


def mixed_row(sums, row):
    total = sums[row]
    channels = total.shape[0] // 2
    total = total[:, :BLOCK] + total[:, BLOCK:]
    return total[:channels] + total[channels:]


def mix_in_body(nodes, cols, ids_ref, total_ref, list_ref, row_ref, pack_ref, *refs):
    pieces, outs = refs[:nodes], refs[nodes : nodes + cols]
    values, sums, store, sem = refs[nodes + cols :]
    one = bring(total_ref, pack_ref, store, sem)
    rows = sums.shape[0]
    node, col = ids_ref[0], ids_ref[1]
    for offset in range(nodes):
        base = (node ^ offset) * rows
        for part in range(rows):
            store_block(values, base + part, pieces[offset][:, part * BLOCK : (part + 1) * BLOCK])
    mix_rows(total_ref, list_ref, row_ref, one, store, values, sums)
    slice_rows = rows // cols
    for offset in range(cols):
        for part in range(slice_rows):
            row = (col ^ offset) * slice_rows + part
            outs[offset][:, part * BLOCK : (part + 1) * BLOCK] = mixed_row(sums, row)


def dense_body(cols, per, ids_ref, *refs):
    pieces, weights = refs[:cols], refs[cols : 2 * cols]
    mixed_ref, hidden_ref, slope_ref, weight_out_ref = refs[2 * cols : 2 * cols + 4]
    outs = refs[2 * cols + 4 : 3 * cols + 4]
    held, held_weights, scores = refs[-3:]
    col = ids_ref[1]
    for offset in range(cols):
        held[col ^ offset] = pieces[offset][...]
        held_weights[col ^ offset] = weights[offset][...]
    feats = held.shape[1]
    units, classes = weight_out_ref.shape
    mixed = held[...].reshape(mixed_ref.shape)
    mixed_ref[...] = mixed
    weight_in = held_weights[:, :feats].reshape(feats * cols, units)
    weight_tail = held_weights[:, feats:].reshape(units, units)
    weight_out_ref[...] = weight_tail[:, :classes]
    inner = product(weight_in, mixed, ((0,), (0,))) + weight_tail[:, classes : classes + 1]
    bend = jnp.tanh(CURVE * (inner + CUBIC * inner * inner * inner))
    hidden = 0.5 * inner * (1.0 + bend)
    hidden_ref[...] = hidden
    slope_ref[...] = 0.5 * (1.0 + bend) + (0.5 * inner) * (1.0 - bend * bend) * (
        CURVE * (1.0 + 3.0 * CUBIC * inner * inner)
    )
    value = product(weight_out_ref[...], hidden, ((0,), (0,)))
    scores[...] = jnp.zeros_like(scores)
    for group in range(cols):
        scores[group, :per] = value[group * per : (group + 1) * per]
    for offset in range(cols):
        outs[offset][...] = scores[col ^ offset]


def stack_body(*refs):
    for index, ref in enumerate(refs[:-1]):
        refs[-1][index] = ref[...]


def mix_out_body(nodes, cols, per, ids_ref, total_ref, list_ref, row_ref, pack_ref, bias_ref, labels_ref, *refs):
    pieces = refs[:nodes]
    logits_ref, stats_ref, values, sums, store, sem = refs[nodes:]
    one = bring(total_ref, pack_ref, store, sem)
    rows = sums.shape[0]
    node, col = ids_ref[0], ids_ref[1]
    slice_rows = rows // cols
    for offset in range(nodes):
        base = (node ^ offset) * rows
        for group in range(cols):
            for part in range(slice_rows):
                store_block(
                    values,
                    base + (col ^ group) * slice_rows + part,
                    pieces[offset][group, :, part * BLOCK : (part + 1) * BLOCK],
                )
    mix_rows(total_ref, list_ref, row_ref, one, store, values, sums)
    for row in range(rows):
        logits_ref[:, row * BLOCK : (row + 1) * BLOCK] = mixed_row(sums, row) + bias_ref[col]
    logits = logits_ref[...]
    place = lax.broadcasted_iota(jnp.int32, logits.shape, 0)
    inside = place < per
    top = jnp.max(jnp.where(inside, logits, -jnp.inf), axis=0, keepdims=True)
    total = jnp.sum(jnp.where(inside, jnp.exp(logits - top), 0.0), axis=0, keepdims=True)
    hit = inside & (place + col * per == labels_ref[...])
    chosen = jnp.sum(jnp.where(hit, logits, 0.0), axis=0, keepdims=True)
    stats_ref[...] = jnp.zeros_like(stats_ref)
    stats_ref[0:1] = top
    stats_ref[1:2] = total
    stats_ref[2:3] = chosen


def mix_back_body(nodes, cols, per, ids_ref, total_ref, list_ref, row_ref, pack_ref, logits_ref, labels_ref, mask_ref, *refs):
    stats, outs = refs[:cols], refs[cols : cols + nodes]
    extra_ref, sums, grads, store, sem = refs[cols + nodes :]
    one = bring(total_ref, pack_ref, store, sem)
    rows = grads.shape[0]
    node, col = ids_ref[0], ids_ref[1]
    tops = [ref[0:1] for ref in stats]
    top = functools.reduce(jnp.maximum, tops)
    total = sum(ref[1:2] * jnp.exp(at - top) for ref, at in zip(stats, tops))
    chosen = sum(ref[2:3] for ref in stats)
    mask = mask_ref[...].astype(f32)
    logits = logits_ref[...]
    place = lax.broadcasted_iota(jnp.int32, logits.shape, 0)
    inside = place < per
    hit = place + col * per == labels_ref[...]
    chance = jnp.exp(logits - top) * (1.0 / total)
    grad = jnp.where(inside, mask * (chance - hit.astype(f32)), 0.0)
    high, low = split(grad)
    ones = jnp.ones((8, grad.shape[1]), bf16)
    bias_row = lax.dot_general(
        ones, high, (((1,), (1,)), ((), ())), preferred_element_type=f32
    ) + lax.dot_general(ones, low, (((1,), (1,)), ((), ())), preferred_element_type=f32)
    loss = jnp.sum(mask * (top + jnp.log(total) - chosen), axis=1, keepdims=True)
    number = jnp.sum(mask, axis=1, keepdims=True)
    first = (col == 0).astype(f32)
    extra_ref[...] = jnp.zeros_like(extra_ref)
    line = lax.broadcasted_iota(jnp.int32, bias_row.shape, 0)
    extra_ref[:, : high.shape[0]] = jnp.where(line == col, bias_row, 0.0)
    extra_ref[cols : cols + 1, 0:1] = loss * first
    extra_ref[cols : cols + 1, 1:2] = number * first

    for row in range(rows):
        at = slice(row * BLOCK, (row + 1) * BLOCK)
        grads[row] = jnp.concatenate(
            [
                jnp.concatenate([high[:, at], high[:, at]], axis=1),
                jnp.concatenate([low[:, at], low[:, at]], axis=1),
            ],
            axis=0,
        )
    sums[...] = jnp.zeros_like(sums)

    def step(group, _):
        one(group).wait()
        for part in range(UNROLL):
            item = group * UNROLL + part
            terms = jnp.dot(grads[row_ref[item]], store[item], preferred_element_type=f32)
            half = terms.shape[0] // 2
            terms = terms[:half] + terms[half:]
            for q in range(CHUNK):
                to = list_ref[item * CHUNK + q]
                sums[to] = sums[to] + terms[:, q * BLOCK : (q + 1) * BLOCK]
        return 0

    lax.fori_loop(0, total_ref[0], step, 0)
    for offset in range(nodes):
        base = (node ^ offset) * rows
        for part in range(rows):
            outs[offset][:, part * BLOCK : (part + 1) * BLOCK] = sums[base + part]


def grads_body(cols, per, ids_ref, mixed_ref, hidden_ref, slope_ref, weight_out_ref, extra_ref, *refs):
    pieces = refs[:cols]
    keep_ref, send_ref, held, packed = refs[cols:]
    core, col = ids_ref[0] & 1, ids_ref[1]
    for offset in range(cols):
        held[col ^ offset] = pieces[offset][...]
    spread = jnp.concatenate([held[group, :per] for group in range(cols)], axis=0)
    classes = spread.shape[0]
    hidden_grad = product(weight_out_ref[...], spread, ((1,), (0,)))
    inner_grad = hidden_grad * slope_ref[...]
    weight_in = product(mixed_ref[...], inner_grad, ((1,), (1,)))
    weight_out = product(hidden_ref[...], spread, ((1,), (1,)))
    bias_in = jnp.sum(inner_grad, axis=1, keepdims=True)
    feats, units = weight_in.shape[0] // cols, weight_out.shape[0] // cols
    packed[...] = jnp.zeros_like(packed)
    for group in range(cols):
        packed[group, :feats] = weight_in[group * feats : (group + 1) * feats]
        rows = slice(group * units, (group + 1) * units)
        packed[group, feats : feats + units, :classes] = weight_out[rows]
        packed[group, feats : feats + units, classes : classes + 1] = bias_in[rows]
        packed[group, feats + units : feats + units + 8] = extra_ref[...]
    half = packed.shape[1] // 2
    for offset in range(cols):
        keep_ref[offset] = packed[col ^ offset, pl.ds(pl.multiple_of(core * half, 8), half)]
        send_ref[offset] = packed[col ^ offset, pl.ds(pl.multiple_of((1 - core) * half, 8), half)]


def finish_body(cols, per, ids_ref, mine_ref, other_ref, weight_in_ref, bias_in_ref, weight_out_ref, bias_out_ref, loss_ref, whole):
    core = ids_ref[0] & 1
    half = mine_ref.shape[0]
    whole[core] = mine_ref[...]
    whole[1 - core] = other_ref[...]
    value = whole[...].reshape(2 * half, mine_ref.shape[1])
    feats, (units, classes) = weight_in_ref.shape[0], weight_out_ref.shape
    weight_in_ref[...] = value[:feats]
    weight_out_ref[...] = value[feats : feats + units, :classes]
    bias_in_ref[...] = value[feats : feats + units, classes : classes + 1]
    extra = value[feats + units : feats + units + 8]
    bias_out_ref[...] = jnp.concatenate([extra[group : group + 1, :per] for group in range(cols)], axis=1)
    loss_ref[...] = extra[cols : cols + 1, 0:1] / jnp.maximum(extra[cols : cols + 1, 1:2], 1.0)


def logits_body(cols, per, ids_ref, *refs):
    pieces, out_ref, held = refs[:cols], refs[cols], refs[-1]
    col = ids_ref[1]
    for offset in range(cols):
        held[col ^ offset] = pieces[offset][...]
    out_ref[...] = jnp.concatenate([held[group, :per] for group in range(cols)], axis=0)


def gather_chips(value, nodes):
    return [value] + [exchange(value, "node", offset) for offset in range(2, nodes, 2)]


def gather_cores(even):
    odd = [exchange(piece, "node", 1) for piece in even]
    return [piece for pair in zip(even, odd) for piece in pair]


def on_device(
    features,
    tiles,
    tile_column,
    tile_count,
    labels,
    train_mask,
    weight_in,
    bias_in,
    weight_out,
    bias_out,
):
    nodes, cols = lax.axis_size("node"), lax.axis_size("col")
    rows = tile_column.shape[0]
    local = labels.shape[0]
    slice_nodes = local // cols
    block_total = nodes * rows
    feats = features.shape[0]
    classes = weight_out.shape[1]
    per = classes // cols
    units = weight_out.shape[0] * cols
    shape = jax.ShapeDtypeStruct
    ids = jnp.stack([lax.axis_index("node"), lax.axis_index("col")]).astype(jnp.int32)

    tail = jnp.concatenate(
        [weight_out, bias_in[:, None], jnp.zeros((units // cols, units - classes - 1), f32)], axis=1
    )
    weights = jnp.concatenate([weight_in, tail], axis=0)
    bias_groups = jnp.pad(bias_out.reshape(cols, per, 1), ((0, 0), (0, PAD - per), (0, 0)))
    labels = labels[None, :]
    train_mask = train_mask[None, :]
    tile_count, ids, bias_groups, labels, train_mask, weights = lax.optimization_barrier(
        (tile_count, ids, bias_groups, labels, train_mask, weights)
    )

    even = gather_chips(features, nodes)
    weight_pieces = [weights] + [exchange(weights, "col", k) for k in range(1, cols)]
    packed, listed, placed, steps = pack(tiles, tile_column, tile_count, block_total)
    steps, *even = lax.optimization_barrier((steps, *even))
    feature_pieces = gather_cores(even)
    sparse = (ids, steps, listed, placed, packed)
    sparse_specs = [SMEM] * 4 + [pl.BlockSpec(memory_space=pltpu.HBM)]
    held = [pltpu.VMEM(packed.shape, bf16), pltpu.SemaphoreType.DMA((packed.shape[0] // UNROLL,))]

    mixed_parts = call(
        functools.partial(mix_in_body, nodes, cols),
        [shape((feats, slice_nodes), f32)] * cols,
        [pltpu.VMEM((block_total, 2 * feats, BLOCK), bf16), pltpu.VMEM((rows, 2 * feats, 2 * BLOCK), f32), *held],
        *sparse,
        *feature_pieces,
        specs=sparse_specs + [VMEM] * nodes,
        limit=44,
        flops=10**9,
        moved=16 * MIB,
    )
    mixed_pieces = [mixed_parts[0]] + [exchange(mixed_parts[k], "col", k) for k in range(1, cols)]
    mixed, hidden, slope, weight_out_all, *score_parts = call(
        functools.partial(dense_body, cols, per),
        [shape((feats * cols, slice_nodes), f32)]
        + [shape((units, slice_nodes), f32)] * 2
        + [shape((units, classes), f32)]
        + [shape((PAD, slice_nodes), f32)] * cols,
        [
            pltpu.VMEM((cols, feats, slice_nodes), f32),
            pltpu.VMEM((cols, *weights.shape), f32),
            pltpu.VMEM((cols, PAD, slice_nodes), f32),
        ],
        ids,
        *mixed_pieces,
        *weight_pieces,
        specs=[SMEM] + [VMEM] * (2 * cols),
        flops=10**8,
        moved=2 * MIB,
    )
    score_pieces = [score_parts[0]] + [exchange(score_parts[k], "col", k) for k in range(1, cols)]
    (stacked,) = call(
        stack_body,
        [shape((cols, PAD, slice_nodes), f32)],
        [],
        *score_pieces,
        limit=4,
        moved=MIB,
    )
    scores = gather_cores(gather_chips(stacked, nodes))
    logits_part, stats = call(
        functools.partial(mix_out_body, nodes, cols, per),
        [shape((PAD, local), f32), shape((8, local), f32)],
        [pltpu.VMEM((block_total, 2 * PAD, BLOCK), bf16), pltpu.VMEM((rows, 2 * PAD, 2 * BLOCK), f32), *held],
        *sparse,
        bias_groups,
        labels,
        *scores,
        specs=sparse_specs + [VMEM] * (2 + nodes),
        limit=44,
        flops=10**9,
        moved=16 * MIB,
    )
    stats_pieces = [stats] + [exchange(stats, "col", k) for k in range(1, cols)]
    *spread_parts, extra = call(
        functools.partial(mix_back_body, nodes, cols, per),
        [shape((PAD, local), f32)] * nodes + [shape((8, 2 * BLOCK), f32)],
        [
            pltpu.VMEM((block_total, PAD, BLOCK), f32),
            pltpu.VMEM((rows, 2 * PAD, 2 * BLOCK), bf16),
            *held,
        ],
        *sparse,
        logits_part,
        labels,
        train_mask,
        *stats_pieces,
        specs=sparse_specs + [VMEM] * (3 + cols),
        limit=44,
        flops=10**9,
        moved=16 * MIB,
    )
    logit_pieces = [logits_part] + [exchange(logits_part, "col", k) for k in range(1, cols)]
    (logits,) = call(
        functools.partial(logits_body, cols, per),
        [shape((classes, local), f32)],
        [pltpu.VMEM((cols, PAD, local), f32)],
        ids,
        *logit_pieces,
        specs=[SMEM] + [VMEM] * cols,
        moved=2 * MIB,
    )

    paired = [
        spread_parts[k] + exchange(spread_parts[k + 1], "node", 1) for k in range(0, nodes, 2)
    ]
    spread = paired[0]
    for index in range(1, nodes // 2):
        spread = spread + exchange(paired[index], "node", 2 * index)
    col = ids[1]
    spread_slices = [
        lax.dynamic_slice_in_dim(spread, (col ^ k) * slice_nodes, slice_nodes, axis=1) for k in range(cols)
    ]
    spread_pieces = [spread_slices[0]] + [exchange(spread_slices[k], "col", k) for k in range(1, cols)]
    logits, *spread_pieces = lax.optimization_barrier((logits, *spread_pieces))

    height = -(-(feats + units // cols + 8) // 16) * 16
    keep, send = call(
        functools.partial(grads_body, cols, per),
        [shape((cols, height // 2, units), f32)] * 2,
        [pltpu.VMEM((cols, PAD, slice_nodes), f32), pltpu.VMEM((cols, height, units), f32)],
        ids,
        mixed,
        hidden,
        slope,
        weight_out_all,
        extra,
        *spread_pieces,
        specs=[SMEM] + [VMEM] * (5 + cols),
        flops=10**8,
        moved=2 * MIB,
    )
    halves = keep + exchange(send, "node", 1)
    total = halves[0]
    for k in range(1, cols):
        total = total + exchange(halves[k], "col", k)
    grand = total
    for k in range(2, nodes, 2):
        grand = grand + exchange(total, "node", k)
    other = exchange(grand, "node", 1)
    grad_in, grad_bias_in, grad_out, grad_bias_out, mean_loss = call(
        functools.partial(finish_body, cols, per),
        [
            shape((feats, units), f32),
            shape((units // cols, 1), f32),
            shape((units // cols, classes), f32),
            shape((1, classes), f32),
            shape((1, 1), f32),
        ],
        [pltpu.VMEM((2, height // 2, units), f32)],
        ids,
        grand,
        other,
        specs=[SMEM, VMEM, VMEM],
    )
    return (logits, mean_loss[0, 0], grad_in, grad_bias_in[:, 0], grad_out, grad_bias_out[0])


def solution(mesh):
    in_specs = (
        P("col", "node"),
        P("node", None, None, None),
        P("node", None),
        P("node"),
        P("node"),
        P("node"),
        P("col", None),
        P("col"),
        P("col", None),
        P(),
    )
    out_specs = (P(None, "node"), P(), P("col", None), P("col"), P("col", None), P())
    return jax.shard_map(
        on_device, mesh=mesh, in_specs=in_specs, out_specs=out_specs, check_vma=False
    )
```

```python
import functools

import jax
import jax.numpy as jnp
from jax import lax
from jax.experimental import pallas as pl
from jax.experimental.pallas import tpu as pltpu
from jax.sharding import PartitionSpec as P

BLOCK = 128
CHUNK = 4
UNROLL = 4
FETCH = 4
RING = 16
PAD = 48
HALF = 24

f32 = jnp.float32
bf16 = jnp.bfloat16
VMEM = pl.BlockSpec(memory_space=pltpu.VMEM)
SMEM = pl.BlockSpec(memory_space=pltpu.SMEM)
MIB = 1 << 20

CURVE = 0.7978845608028654
CUBIC = 0.044715


def exchange(value, axis, offset):
    total = lax.axis_size(axis)
    return lax.ppermute(value, axis, [(i, i ^ offset) for i in range(total)])


def split(value):
    high = value.astype(bf16)
    low = (value - high.astype(f32)).astype(bf16)
    return high, low


def product(left, right, dims):
    lh, ll = split(left)
    rh, rl = split(right)

    def one(a, b):
        return lax.dot_general(a, b, (dims, ((), ())), preferred_element_type=f32)

    return one(lh, rh) + (one(lh, rl) + one(ll, rh))


def call(body, outs, scratch, *args, specs=None, out_specs=None, limit=12, flops=0, moved=0):
    return pl.pallas_call(
        body,
        out_shape=outs,
        in_specs=specs or [VMEM] * len(args),
        out_specs=out_specs or [VMEM] * len(outs),
        scratch_shapes=scratch,
        compiler_params=pltpu.CompilerParams(vmem_limit_bytes=limit * MIB),
        cost_estimate=pl.CostEstimate(flops=flops, bytes_accessed=moved, transcendentals=0),
    )(*args)


def as_column(row):
    size = row.shape[1]
    shape = (size, size)
    same = lax.broadcasted_iota(jnp.int32, shape, 0) == lax.broadcasted_iota(jnp.int32, shape, 1)
    return jnp.sum(jnp.where(same, row, 0.0), axis=1, keepdims=True)


def as_row(column):
    size = column.shape[0]
    shape = (size, size)
    same = lax.broadcasted_iota(jnp.int32, shape, 0) == lax.broadcasted_iota(jnp.int32, shape, 1)
    return jnp.sum(jnp.where(same, column, 0.0), axis=0, keepdims=True)


def pack_body(
    count_in, column_in, tiles_ref, pack_ref, list_ref, row_ref, total_ref,
    count_ref, column_ref, land, store, place, owner, twin_from, twin_to, sem, out_sem, list_sem,
):
    rows, slots = column_ref.shape
    lists = [
        pltpu.make_async_copy(count_in, count_ref, list_sem.at[0]),
        pltpu.make_async_copy(column_in, column_ref, list_sem.at[1]),
    ]
    for copy in lists:
        copy.start()
    for copy in lists:
        copy.wait()

    def copies(row, act):
        def one(group, _):
            part = pl.ds(group * FETCH, FETCH)
            copy = pltpu.make_async_copy(
                tiles_ref.at[row, part], land.at[pl.ds(row * slots + group * FETCH, FETCH)], sem.at[row, group]
            )
            act(copy)
            return 0

        lax.fori_loop(0, (count_ref[row] + FETCH - 1) // FETCH, one, 0)

    def leave(item):
        return pltpu.make_async_copy(store.at[lax.rem(item, RING)], pack_ref.at[item], out_sem.at[lax.rem(item, RING)])

    def free(item):
        @pl.when(item >= RING)
        def _():
            leave(item - RING).wait()

    def start(copy):
        copy.start()

    def wait(copy):
        copy.wait()

    for row in range(rows):
        copies(row, start)
    land[rows * slots] = jnp.zeros((BLOCK, BLOCK), f32)

    def clear(index, _):
        place[index] = -1
        return 0

    lax.fori_loop(0, place.shape[0], clear, 0)

    def one_row(row, begin):
        stamp = row * slots

        def scan(slot, state):
            found, twins = state
            column = column_ref[row, slot]
            at = place[column]
            fresh = at < stamp

            @pl.when(fresh)
            def _():
                place[column] = stamp + slot
                owner[found] = stamp + slot
                list_ref[begin * CHUNK + found] = column

            @pl.when(jnp.logical_not(fresh))
            def _():
                twin_from[twins] = stamp + slot
                twin_to[twins] = at

            step = fresh.astype(jnp.int32)
            return found + step, twins + 1 - step

        found, twins = lax.fori_loop(0, count_ref[row], scan, (0, 0))
        steps = (found + CHUNK - 1) // CHUNK

        def blank(index, _):
            list_ref[begin * CHUNK + index] = 0
            owner[index] = rows * slots
            return 0

        lax.fori_loop(found, steps * CHUNK, blank, 0)
        copies(row, wait)

        def join(index, _):
            to = twin_to[index]
            land[to] = land[to] + land[twin_from[index]]
            return 0

        lax.fori_loop(0, twins, join, 0)

        def convert(step, _):
            item = begin + step
            row_ref[item] = row
            free(item)
            place_at = lax.rem(item, RING)
            for q in range(CHUNK):
                at = slice(q * BLOCK, (q + 1) * BLOCK)
                high, low = split(land[owner[step * CHUNK + q]])
                store[place_at, :BLOCK, at] = high
                store[place_at, BLOCK:, at] = low
            leave(item).start()
            return 0

        lax.fori_loop(0, steps, convert, 0)

        return begin + steps

    used = lax.fori_loop(0, rows, one_row, 0)
    total = (used + UNROLL - 1) // UNROLL * UNROLL

    def fill(item, _):
        row_ref[item] = 0
        for q in range(CHUNK):
            list_ref[item * CHUNK + q] = 0
        free(item)
        store[lax.rem(item, RING)] = jnp.zeros(store.shape[1:], bf16)
        leave(item).start()
        return 0

    lax.fori_loop(used, total, fill, 0)
    total_ref[0] = total // UNROLL

    def last(item, _):
        leave(item).wait()
        return 0

    lax.fori_loop(jnp.maximum(total - RING, 0), total, last, 0)


def pack(tiles, tile_column, tile_count, block_total):
    rows, slots = tile_column.shape
    items = -(-rows * slots // (CHUNK * UNROLL)) * UNROLL
    shape = jax.ShapeDtypeStruct
    return call(
        pack_body,
        [
            pltpu.HBM((items, 2 * BLOCK, CHUNK * BLOCK), bf16),
            shape((items * CHUNK,), jnp.int32),
            shape((items,), jnp.int32),
            shape((1,), jnp.int32),
        ],
        [
            pltpu.SMEM(tile_count.shape, jnp.int32),
            pltpu.SMEM(tile_column.shape, jnp.int32),
            pltpu.VMEM((rows * slots + 1, BLOCK, BLOCK), f32),
            pltpu.VMEM((RING, 2 * BLOCK, CHUNK * BLOCK), bf16),
            pltpu.SMEM((block_total,), jnp.int32),
            pltpu.SMEM((slots,), jnp.int32),
            pltpu.SMEM((slots,), jnp.int32),
            pltpu.SMEM((slots,), jnp.int32),
            pltpu.SemaphoreType.DMA((rows, slots // FETCH)),
            pltpu.SemaphoreType.DMA((RING,)),
            pltpu.SemaphoreType.DMA((2,)),
        ],
        tile_count,
        tile_column,
        tiles,
        specs=[pl.BlockSpec(memory_space=pl.ANY)] * 3,
        out_specs=[pl.BlockSpec(memory_space=pltpu.HBM), SMEM, SMEM, SMEM],
        limit=52,
        flops=10**8,
        moved=40 * MIB,
    )


def bring(total_ref, pack_ref, store, sem):
    def one(group):
        part = pl.ds(group * UNROLL, UNROLL)
        return pltpu.make_async_copy(pack_ref.at[part], store.at[part], sem.at[group])

    def start(group, _):
        one(group).start()
        return 0

    lax.fori_loop(0, total_ref[0], start, 0)
    return one


def store_block(values, at, value):
    channels = value.shape[0]
    high, low = split(value)
    values[at, :channels] = high
    values[at, channels:] = low


def mix_rows(total_ref, list_ref, row_ref, one, store, values, sums):
    sums[...] = jnp.zeros_like(sums)

    def step(group, _):
        one(group).wait()
        for part in range(UNROLL):
            item = group * UNROLL + part
            left = jnp.concatenate([values[list_ref[item * CHUNK + q]] for q in range(CHUNK)], axis=1)
            row = row_ref[item]
            sums[row] = sums[row] + lax.dot_general(
                left, store[item], (((1,), (1,)), ((), ())), preferred_element_type=f32
            )
        return 0

    lax.fori_loop(0, total_ref[0], step, 0)


def mixed_row(sums, row):
    total = sums[row]
    channels = total.shape[0] // 2
    total = total[:, :BLOCK] + total[:, BLOCK:]
    return total[:channels] + total[channels:]


def mix_in_body(nodes, cols, ids_ref, total_ref, list_ref, row_ref, pack_ref, *refs):
    pieces, outs = refs[:nodes], refs[nodes : nodes + cols]
    values, sums, store, sem = refs[nodes + cols :]
    one = bring(total_ref, pack_ref, store, sem)
    rows = sums.shape[0]
    node, col = ids_ref[0], ids_ref[1]
    for offset in range(nodes):
        base = (node ^ offset) * rows
        for part in range(rows):
            store_block(values, base + part, pieces[offset][:, part * BLOCK : (part + 1) * BLOCK])
    mix_rows(total_ref, list_ref, row_ref, one, store, values, sums)
    slice_rows = rows // cols
    for offset in range(cols):
        for part in range(slice_rows):
            row = (col ^ offset) * slice_rows + part
            outs[offset][:, part * BLOCK : (part + 1) * BLOCK] = mixed_row(sums, row)


def dense_body(cols, per, ids_ref, *refs):
    pieces, weights = refs[:cols], refs[cols : 2 * cols]
    mixed_ref, hidden_ref, slope_ref, weight_out_ref = refs[2 * cols : 2 * cols + 4]
    outs = refs[2 * cols + 4 : 3 * cols + 4]
    held, held_weights, scores = refs[-3:]
    col = ids_ref[1]
    for offset in range(cols):
        held[col ^ offset] = pieces[offset][...]
        held_weights[col ^ offset] = weights[offset][...]
    feats = held.shape[1]
    units, classes = weight_out_ref.shape
    mixed = held[...].reshape(mixed_ref.shape)
    mixed_ref[...] = mixed
    weight_in = held_weights[:, :feats].reshape(feats * cols, units)
    own = units // cols
    weight_out = held_weights[:, feats : feats + own].reshape(units, units)[:, :classes]
    weight_out_ref[...] = weight_out
    bias_in = jnp.concatenate(
        [held_weights[group, feats + own : feats + own + 1, :own] for group in range(cols)], axis=1
    )
    inner = product(weight_in, mixed, ((0,), (0,))) + as_column(bias_in)
    bend = jnp.tanh(CURVE * (inner + CUBIC * inner * inner * inner))
    hidden = 0.5 * inner * (1.0 + bend)
    hidden_ref[...] = hidden
    slope_ref[...] = 0.5 * (1.0 + bend) + (0.5 * inner) * (1.0 - bend * bend) * (
        CURVE * (1.0 + 3.0 * CUBIC * inner * inner)
    )
    value = product(weight_out, hidden, ((0,), (0,)))
    scores[...] = jnp.zeros_like(scores)
    for group in range(cols):
        scores[group, :per] = value[group * per : (group + 1) * per]
    for offset in range(cols):
        outs[offset][...] = scores[col ^ offset]


def stack_body(*refs):
    for index, ref in enumerate(refs[:-1]):
        refs[-1][index] = ref[...]


def mix_out_body(nodes, cols, per, ids_ref, total_ref, list_ref, row_ref, pack_ref, bias_ref, labels_ref, *refs):
    pieces = refs[:nodes]
    upper_ref, lower_ref, stats_ref, values, sums, groups, store, sem = refs[nodes:]
    one = bring(total_ref, pack_ref, store, sem)
    rows = sums.shape[0]
    node, col = ids_ref[0], ids_ref[1]
    slice_rows = rows // cols
    column = as_column(bias_ref[...])
    groups[...] = jnp.zeros_like(groups)
    for group in range(cols):
        groups[group, :per] = column[group * per : (group + 1) * per]
    for offset in range(nodes):
        base = (node ^ offset) * rows
        for group in range(cols):
            for part in range(slice_rows):
                store_block(
                    values,
                    base + (col ^ group) * slice_rows + part,
                    pieces[offset][group, :, part * BLOCK : (part + 1) * BLOCK],
                )
    mix_rows(total_ref, list_ref, row_ref, one, store, values, sums)
    for row in range(rows):
        at = slice(row * BLOCK, (row + 1) * BLOCK)
        total = mixed_row(sums, row) + groups[col]
        upper_ref[:, at] = total[:HALF]
        lower_ref[:, at] = total[HALF:]
    logits = jnp.concatenate([upper_ref[...], lower_ref[...]], axis=0)
    place = lax.broadcasted_iota(jnp.int32, logits.shape, 0)
    inside = place < per
    top = jnp.max(jnp.where(inside, logits, -jnp.inf), axis=0, keepdims=True)
    total = jnp.sum(jnp.where(inside, jnp.exp(logits - top), 0.0), axis=0, keepdims=True)
    hit = inside & (place + col * per == labels_ref[...])
    chosen = jnp.sum(jnp.where(hit, logits, 0.0), axis=0, keepdims=True)
    stats_ref[...] = jnp.zeros_like(stats_ref)
    stats_ref[0:1] = top
    stats_ref[1:2] = total
    stats_ref[2:3] = chosen


def mix_back_body(nodes, cols, per, ids_ref, total_ref, list_ref, row_ref, pack_ref, upper_ref, lower_ref, labels_ref, mask_ref, *refs):
    stats, outs = refs[:cols], refs[cols : cols + nodes]
    extra_ref, sums, grads, store, sem = refs[cols + nodes :]
    one = bring(total_ref, pack_ref, store, sem)
    rows = grads.shape[0]
    node, col = ids_ref[0], ids_ref[1]
    tops = [ref[0:1] for ref in stats]
    top = functools.reduce(jnp.maximum, tops)
    total = sum(ref[1:2] * jnp.exp(at - top) for ref, at in zip(stats, tops))
    chosen = sum(ref[2:3] for ref in stats)
    mask = mask_ref[...].astype(f32)
    logits = jnp.concatenate([upper_ref[...], lower_ref[...]], axis=0)
    place = lax.broadcasted_iota(jnp.int32, logits.shape, 0)
    inside = place < per
    hit = place + col * per == labels_ref[...]
    chance = jnp.exp(logits - top) * (1.0 / total)
    grad = jnp.where(inside, mask * (chance - hit.astype(f32)), 0.0)
    high, low = split(grad)
    ones = jnp.ones((8, grad.shape[1]), bf16)
    bias_row = lax.dot_general(
        ones, high, (((1,), (1,)), ((), ())), preferred_element_type=f32
    ) + lax.dot_general(ones, low, (((1,), (1,)), ((), ())), preferred_element_type=f32)
    loss = jnp.sum(mask * (top + jnp.log(total) - chosen), axis=1, keepdims=True)
    number = jnp.sum(mask, axis=1, keepdims=True)
    first = (col == 0).astype(f32)
    extra_ref[...] = jnp.zeros_like(extra_ref)
    line = lax.broadcasted_iota(jnp.int32, bias_row.shape, 0)
    extra_ref[:, : high.shape[0]] = jnp.where(line == col, bias_row, 0.0)
    extra_ref[cols : cols + 1, 0:1] = loss * first
    extra_ref[cols : cols + 1, 1:2] = number * first

    for row in range(rows):
        at = slice(row * BLOCK, (row + 1) * BLOCK)
        grads[row] = jnp.concatenate(
            [
                jnp.concatenate([high[:, at], high[:, at]], axis=1),
                jnp.concatenate([low[:, at], low[:, at]], axis=1),
            ],
            axis=0,
        )
    sums[...] = jnp.zeros_like(sums)

    def step(group, _):
        one(group).wait()
        for part in range(UNROLL):
            item = group * UNROLL + part
            terms = jnp.dot(grads[row_ref[item]], store[item], preferred_element_type=f32)
            half = terms.shape[0] // 2
            terms = terms[:half] + terms[half:]
            for q in range(CHUNK):
                to = list_ref[item * CHUNK + q]
                sums[to] = sums[to] + terms[:, q * BLOCK : (q + 1) * BLOCK]
        return 0

    lax.fori_loop(0, total_ref[0], step, 0)
    for offset in range(nodes):
        base = (node ^ offset) * rows
        for part in range(rows):
            outs[offset][:, part * BLOCK : (part + 1) * BLOCK] = sums[base + part]


def pair_body(*refs):
    count = len(refs) // 3
    for index in range(count):
        refs[2 * count + index][...] = refs[index][...] + refs[count + index][...]


def sum_body(cols, ids_ref, *refs):
    parts, outs, held = refs[: -cols - 1], refs[-cols - 1 : -1], refs[-1]
    col = ids_ref[1]
    total = sum((ref[...] for ref in parts[1:]), parts[0][...])
    width = total.shape[1] // cols
    for group in range(cols):
        held[group] = total[:, group * width : (group + 1) * width]
    for offset in range(cols):
        outs[offset][...] = held[col ^ offset]


def grads_body(cols, per, ids_ref, mixed_ref, hidden_ref, slope_ref, weight_out_ref, extra_ref, *refs):
    pieces = refs[:cols]
    keep_ref, send_ref, held, packed = refs[cols:]
    core, col = ids_ref[0] & 1, ids_ref[1]
    for offset in range(cols):
        held[col ^ offset] = pieces[offset][...]
    spread = jnp.concatenate([held[group, :per] for group in range(cols)], axis=0)
    classes = spread.shape[0]
    hidden_grad = product(weight_out_ref[...], spread, ((1,), (0,)))
    inner_grad = hidden_grad * slope_ref[...]
    weight_in = product(mixed_ref[...], inner_grad, ((1,), (1,)))
    weight_out = product(hidden_ref[...], spread, ((1,), (1,)))
    bias_in = jnp.sum(inner_grad, axis=1, keepdims=True)
    feats, units = weight_in.shape[0] // cols, weight_out.shape[0] // cols
    packed[...] = jnp.zeros_like(packed)
    for group in range(cols):
        packed[group, :feats] = weight_in[group * feats : (group + 1) * feats]
        rows = slice(group * units, (group + 1) * units)
        packed[group, feats : feats + units, :classes] = weight_out[rows]
        packed[group, feats : feats + units, classes : classes + 1] = bias_in[rows]
        packed[group, feats + units : feats + units + 8] = extra_ref[...]
    half = packed.shape[1] // 2
    for offset in range(cols):
        keep_ref[offset] = packed[col ^ offset, pl.ds(pl.multiple_of(core * half, 8), half)]
        send_ref[offset] = packed[col ^ offset, pl.ds(pl.multiple_of((1 - core) * half, 8), half)]


def finish_body(cols, per, ids_ref, mine_ref, other_ref, weight_in_ref, bias_in_ref, weight_out_ref, bias_out_ref, loss_ref, whole):
    core = ids_ref[0] & 1
    half = mine_ref.shape[0]
    whole[core] = mine_ref[...]
    whole[1 - core] = other_ref[...]
    value = whole[...].reshape(2 * half, mine_ref.shape[1])
    feats, (units, classes) = weight_in_ref.shape[0], weight_out_ref.shape
    weight_in_ref[...] = value[:feats]
    weight_out_ref[...] = value[feats : feats + units, :classes]
    bias_in_ref[...] = as_row(value[feats : feats + units, classes : classes + 1])
    extra = value[feats + units : feats + units + 8]
    bias_out_ref[...] = jnp.concatenate([extra[group : group + 1, :per] for group in range(cols)], axis=1)
    loss_ref[...] = extra[cols : cols + 1, 0:1] / jnp.maximum(extra[cols : cols + 1, 1:2], 1.0)


def logits_body(cols, per, ids_ref, *refs):
    uppers, lowers, out_ref, held = refs[:cols], refs[cols : 2 * cols], refs[-2], refs[-1]
    col = ids_ref[1]
    for offset in range(cols):
        held[col ^ offset, :HALF] = uppers[offset][...]
        held[col ^ offset, HALF:] = lowers[offset][...]
    out_ref[...] = jnp.concatenate([held[group, :per] for group in range(cols)], axis=0)


def gather_chips(value, nodes):
    return [value] + [exchange(value, "node", offset) for offset in range(2, nodes, 2)]


def gather_cores(even):
    odd = [exchange(piece, "node", 1) for piece in even]
    return [piece for pair in zip(even, odd) for piece in pair]


def on_device(
    features,
    tiles,
    tile_column,
    tile_count,
    labels,
    train_mask,
    weight_in,
    bias_in,
    weight_out,
    bias_out,
):
    nodes, cols = lax.axis_size("node"), lax.axis_size("col")
    rows = tile_column.shape[0]
    local = labels.shape[0]
    slice_nodes = local // cols
    block_total = nodes * rows
    feats = features.shape[0]
    classes = weight_out.shape[1]
    per = classes // cols
    units = weight_out.shape[0] * cols
    shape = jax.ShapeDtypeStruct
    ids = jnp.stack([lax.axis_index("node"), lax.axis_index("col")]).astype(jnp.int32)

    labels = labels[None, :]
    train_mask = train_mask[None, :]
    own = units // cols
    height = feats + own + 8
    weights = (
        jnp.pad(weight_in, ((0, height - feats), (0, 0)))
        + jnp.pad(weight_out, ((feats, 8), (0, units - classes)))
        + jnp.pad(bias_in[None, :], ((feats + own, 7), (0, units - own)))
    )
    even = gather_chips(features, nodes)
    weight_pieces = [weights] + [exchange(weights, "col", k) for k in range(1, cols)]
    packed, listed, placed, steps = pack(tiles, tile_column, tile_count, block_total)
    steps, even, weight_pieces = lax.optimization_barrier((steps, even, weight_pieces))
    feature_pieces = gather_cores(even)
    sparse = (ids, steps, listed, placed, packed)
    sparse_specs = [SMEM] * 4 + [pl.BlockSpec(memory_space=pltpu.HBM)]
    held = [pltpu.VMEM(packed.shape, bf16), pltpu.SemaphoreType.DMA((packed.shape[0] // UNROLL,))]

    mixed_parts = call(
        functools.partial(mix_in_body, nodes, cols),
        [shape((feats, slice_nodes), f32)] * cols,
        [pltpu.VMEM((block_total, 2 * feats, BLOCK), bf16), pltpu.VMEM((rows, 2 * feats, 2 * BLOCK), f32), *held],
        *sparse,
        *feature_pieces,
        specs=sparse_specs + [VMEM] * nodes,
        limit=44,
        flops=10**9,
        moved=16 * MIB,
    )
    mixed_pieces = [mixed_parts[0]] + [exchange(mixed_parts[k], "col", k) for k in range(1, cols)]
    mixed, hidden, slope, weight_out_all, *score_parts = call(
        functools.partial(dense_body, cols, per),
        [shape((feats * cols, slice_nodes), f32)]
        + [shape((units, slice_nodes), f32)] * 2
        + [shape((units, classes), f32)]
        + [shape((PAD, slice_nodes), f32)] * cols,
        [
            pltpu.VMEM((cols, feats, slice_nodes), f32),
            pltpu.VMEM((cols, *weights.shape), f32),
            pltpu.VMEM((cols, PAD, slice_nodes), f32),
        ],
        ids,
        *mixed_pieces,
        *weight_pieces,
        specs=[SMEM] + [VMEM] * (2 * cols),
        flops=10**8,
        moved=2 * MIB,
    )
    score_pieces = [score_parts[0]] + [exchange(score_parts[k], "col", k) for k in range(1, cols)]
    (stacked,) = call(
        stack_body,
        [shape((cols, PAD, slice_nodes), f32)],
        [],
        *score_pieces,
        limit=4,
        moved=MIB,
    )
    scores = gather_cores(gather_chips(stacked, nodes))
    upper, lower, stats = call(
        functools.partial(mix_out_body, nodes, cols, per),
        [shape((HALF, local), f32), shape((PAD - HALF, local), f32), shape((8, local), f32)],
        [pltpu.VMEM((block_total, 2 * PAD, BLOCK), bf16), pltpu.VMEM((rows, 2 * PAD, 2 * BLOCK), f32), pltpu.VMEM((cols, PAD, 1), f32), *held],
        *sparse,
        bias_out[None, :],
        labels,
        *scores,
        specs=sparse_specs + [VMEM] * (2 + nodes),
        limit=44,
        flops=10**9,
        moved=16 * MIB,
    )
    stats_pieces = [stats] + [exchange(stats, "col", k) for k in range(1, cols)]
    *spread_parts, extra = call(
        functools.partial(mix_back_body, nodes, cols, per),
        [shape((PAD, local), f32)] * nodes + [shape((8, 2 * BLOCK), f32)],
        [
            pltpu.VMEM((block_total, PAD, BLOCK), f32),
            pltpu.VMEM((rows, 2 * PAD, 2 * BLOCK), bf16),
            *held,
        ],
        *sparse,
        upper,
        lower,
        labels,
        train_mask,
        *stats_pieces,
        specs=sparse_specs + [VMEM] * (4 + cols),
        limit=44,
        flops=10**9,
        moved=16 * MIB,
    )
    uppers = [upper] + [exchange(upper, "col", k) for k in range(1, cols)]
    spread_parts, uppers = lax.optimization_barrier((spread_parts, uppers))
    paired = call(
        pair_body,
        [shape((PAD, local), f32)] * (nodes // 2),
        [],
        *spread_parts[::2],
        *[exchange(part, "node", 1) for part in spread_parts[1::2]],
        limit=8,
        moved=2 * MIB,
    )
    paired, lower = lax.optimization_barrier((paired, lower))
    chips = [exchange(paired[k], "node", 2 * k) for k in range(1, nodes // 2)]
    lowers = [lower] + [exchange(lower, "col", k) for k in range(1, cols)]
    spread_slices = call(
        functools.partial(sum_body, cols),
        [shape((PAD, slice_nodes), f32)] * cols,
        [pltpu.VMEM((cols, PAD, slice_nodes), f32)],
        ids,
        paired[0],
        *chips,
        specs=[SMEM] + [VMEM] * (nodes // 2),
        limit=8,
        moved=MIB,
    )
    spread_slices, lowers = lax.optimization_barrier((spread_slices, lowers))
    spread_pieces = [spread_slices[0]] + [exchange(spread_slices[k], "col", k) for k in range(1, cols)]
    (logits,) = call(
        functools.partial(logits_body, cols, per),
        [shape((classes, local), f32)],
        [pltpu.VMEM((cols, PAD, local), f32)],
        ids,
        *uppers,
        *lowers,
        specs=[SMEM] + [VMEM] * (2 * cols),
        limit=8,
        moved=2 * MIB,
    )
    logits, *spread_pieces = lax.optimization_barrier((logits, *spread_pieces))

    height = -(-(feats + units // cols + 8) // 16) * 16
    keep, send = call(
        functools.partial(grads_body, cols, per),
        [shape((cols, height // 2, units), f32)] * 2,
        [pltpu.VMEM((cols, PAD, slice_nodes), f32), pltpu.VMEM((cols, height, units), f32)],
        ids,
        mixed,
        hidden,
        slope,
        weight_out_all,
        extra,
        *spread_pieces,
        specs=[SMEM] + [VMEM] * (5 + cols),
        flops=10**8,
        moved=2 * MIB,
    )
    halves = keep + exchange(send, "node", 1)
    total = halves[0]
    for k in range(1, cols):
        total = total + exchange(halves[k], "col", k)
    grand = total
    for k in range(2, nodes, 2):
        grand = grand + exchange(total, "node", k)
    other = exchange(grand, "node", 1)
    grad_in, grad_bias_in, grad_out, grad_bias_out, mean_loss = call(
        functools.partial(finish_body, cols, per),
        [
            shape((feats, units), f32),
            shape((1, units // cols), f32),
            shape((units // cols, classes), f32),
            shape((1, classes), f32),
            shape((1, 1), f32),
        ],
        [pltpu.VMEM((2, height // 2, units), f32)],
        ids,
        grand,
        other,
        specs=[SMEM, VMEM, VMEM],
    )
    return (
        logits,
        mean_loss.reshape(()),
        grad_in,
        grad_bias_in.reshape(-1),
        grad_out,
        grad_bias_out.reshape(-1),
    )


def solution(mesh):
    in_specs = (
        P("col", "node"),
        P("node", None, None, None),
        P("node", None),
        P("node"),
        P("node"),
        P("node"),
        P("col", None),
        P("col"),
        P("col", None),
        P(),
    )
    out_specs = (P(None, "node"), P(), P("col", None), P("col"), P("col", None), P())
    return jax.shard_map(
        on_device, mesh=mesh, in_specs=in_specs, out_specs=out_specs, check_vma=False
    )
```

```python
import functools

import jax
import jax.numpy as jnp
from jax import lax
from jax.experimental import pallas as pl
from jax.experimental.pallas import tpu as pltpu
from jax.sharding import PartitionSpec as P

BLOCK = 128
CHUNK = 4
UNROLL = 4
FETCH = 4
DEPTH = 3
PAD = 48
HALF = 24

f32 = jnp.float32
bf16 = jnp.bfloat16
VMEM = pl.BlockSpec(memory_space=pltpu.VMEM)
SMEM = pl.BlockSpec(memory_space=pltpu.SMEM)
MIB = 1 << 20

CURVE = 0.7978845608028654
CUBIC = 0.044715


def exchange(value, axis, offset):
    total = lax.axis_size(axis)
    return lax.ppermute(value, axis, [(i, i ^ offset) for i in range(total)])


def split(value):
    high = value.astype(bf16)
    low = (value - high.astype(f32)).astype(bf16)
    return high, low


def product(left, right, dims):
    lh, ll = split(left)
    rh, rl = split(right)

    def one(a, b):
        return lax.dot_general(a, b, (dims, ((), ())), preferred_element_type=f32)

    return one(lh, rh) + (one(lh, rl) + one(ll, rh))


def call(body, outs, scratch, *args, specs=None, out_specs=None, limit=20, flops=0, moved=0):
    return pl.pallas_call(
        body,
        out_shape=outs,
        in_specs=specs or [VMEM] * len(args),
        out_specs=out_specs or [VMEM] * len(outs),
        scratch_shapes=scratch,
        compiler_params=pltpu.CompilerParams(vmem_limit_bytes=limit * MIB),
        cost_estimate=pl.CostEstimate(flops=flops, bytes_accessed=moved, transcendentals=0),
    )(*args)


def as_column(row):
    size = row.shape[1]
    shape = (size, size)
    same = lax.broadcasted_iota(jnp.int32, shape, 0) == lax.broadcasted_iota(jnp.int32, shape, 1)
    return jnp.sum(jnp.where(same, row, 0.0), axis=1, keepdims=True)


def as_row(column):
    size = column.shape[0]
    shape = (size, size)
    same = lax.broadcasted_iota(jnp.int32, shape, 0) == lax.broadcasted_iota(jnp.int32, shape, 1)
    return jnp.sum(jnp.where(same, column, 0.0), axis=0, keepdims=True)


def pack_body(
    count_in, column_in, tiles_ref, pack_ref, list_ref, row_ref, total_ref,
    count_ref, column_ref, land, place, owner, twin_from, twin_to, sem, list_sem,
):
    rows, slots = column_ref.shape
    lists = [
        pltpu.make_async_copy(count_in, count_ref, list_sem.at[0]),
        pltpu.make_async_copy(column_in, column_ref, list_sem.at[1]),
    ]
    for copy in lists:
        copy.start()
    for copy in lists:
        copy.wait()

    def copies(row, act):
        ring = lax.rem(row, DEPTH)

        def one(group, _):
            part = pl.ds(group * FETCH, FETCH)
            copy = pltpu.make_async_copy(
                tiles_ref.at[row, part], land.at[pl.ds(ring * slots + group * FETCH, FETCH)], sem.at[ring, group]
            )
            act(copy)
            return 0

        lax.fori_loop(0, (count_ref[row] + FETCH - 1) // FETCH, one, 0)

    def start(copy):
        copy.start()

    def wait(copy):
        copy.wait()

    for row in range(DEPTH):
        copies(row, start)
    land[DEPTH * slots] = jnp.zeros((BLOCK, BLOCK), f32)

    def clear(index, _):
        place[index] = -1
        return 0

    lax.fori_loop(0, place.shape[0], clear, 0)

    def one_row(row, begin):
        stamp = row * slots
        shift = stamp - lax.rem(row, DEPTH) * slots

        def scan(slot, state):
            found, twins = state
            column = column_ref[row, slot]
            at = place[column]
            fresh = at < stamp

            @pl.when(fresh)
            def _():
                place[column] = stamp + slot
                owner[found] = stamp - shift + slot
                list_ref[begin * CHUNK + found] = column

            @pl.when(jnp.logical_not(fresh))
            def _():
                twin_from[twins] = stamp - shift + slot
                twin_to[twins] = at - shift

            step = fresh.astype(jnp.int32)
            return found + step, twins + 1 - step

        found, twins = lax.fori_loop(0, count_ref[row], scan, (0, 0))
        steps = (found + CHUNK - 1) // CHUNK

        def blank(index, _):
            list_ref[begin * CHUNK + index] = 0
            owner[index] = DEPTH * slots
            return 0

        lax.fori_loop(found, steps * CHUNK, blank, 0)
        copies(row, wait)

        def join(index, _):
            to = twin_to[index]
            land[to] = land[to] + land[twin_from[index]]
            return 0

        lax.fori_loop(0, twins, join, 0)

        def convert(step, _):
            item = begin + step
            row_ref[item] = row
            for q in range(CHUNK):
                at = slice(q * BLOCK, (q + 1) * BLOCK)
                high, low = split(land[owner[step * CHUNK + q]])
                pack_ref[item, :BLOCK, at] = high
                pack_ref[item, BLOCK:, at] = low
            return 0

        lax.fori_loop(0, steps, convert, 0)

        @pl.when(row + DEPTH < rows)
        def _():
            copies(row + DEPTH, start)

        return begin + steps

    used = lax.fori_loop(0, rows, one_row, 0)
    total = (used + UNROLL - 1) // UNROLL * UNROLL

    def fill(item, _):
        row_ref[item] = 0
        for q in range(CHUNK):
            list_ref[item * CHUNK + q] = 0
        pack_ref[item] = jnp.zeros(pack_ref.shape[1:], bf16)
        return 0

    lax.fori_loop(used, total, fill, 0)
    total_ref[0] = total // UNROLL


def pack(tiles, tile_column, tile_count, block_total):
    rows, slots = tile_column.shape
    items = -(-rows * slots // (CHUNK * UNROLL)) * UNROLL
    shape = jax.ShapeDtypeStruct
    return call(
        pack_body,
        [
            pltpu.VMEM((items, 2 * BLOCK, CHUNK * BLOCK), bf16),
            shape((items * CHUNK,), jnp.int32),
            shape((items,), jnp.int32),
            shape((1,), jnp.int32),
        ],
        [
            pltpu.SMEM(tile_count.shape, jnp.int32),
            pltpu.SMEM(tile_column.shape, jnp.int32),
            pltpu.VMEM((DEPTH * slots + 1, BLOCK, BLOCK), f32),
            pltpu.SMEM((block_total,), jnp.int32),
            pltpu.SMEM((slots,), jnp.int32),
            pltpu.SMEM((slots,), jnp.int32),
            pltpu.SMEM((slots,), jnp.int32),
            pltpu.SemaphoreType.DMA((DEPTH, slots // FETCH)),
            pltpu.SemaphoreType.DMA((2,)),
        ],
        pltpu.with_memory_space_constraint(tile_count, pltpu.HBM),
        pltpu.with_memory_space_constraint(tile_column, pltpu.HBM),
        tiles,
        specs=[pl.BlockSpec(memory_space=pl.ANY)] * 3,
        out_specs=[VMEM, SMEM, SMEM, SMEM],
        limit=20,
        flops=10**8,
        moved=40 * MIB,
    )


def bring(total_ref, pack_ref, store, sem):
    def one(group):
        part = pl.ds(group * UNROLL, UNROLL)
        return pltpu.make_async_copy(pack_ref.at[part], store.at[part], sem.at[group])

    def start(group, _):
        one(group).start()
        return 0

    lax.fori_loop(0, total_ref[0], start, 0)
    return one


def store_block(values, at, value):
    channels = value.shape[0]
    high, low = split(value)
    values[at, :channels] = high
    values[at, channels:] = low


def mix_rows(total_ref, list_ref, row_ref, store, values, sums):
    sums[...] = jnp.zeros_like(sums)

    def step(group, _):
        for part in range(UNROLL):
            item = group * UNROLL + part
            left = jnp.concatenate([values[list_ref[item * CHUNK + q]] for q in range(CHUNK)], axis=1)
            row = row_ref[item]
            sums[row] = sums[row] + lax.dot_general(
                left, store[item], (((1,), (1,)), ((), ())), preferred_element_type=f32
            )
        return 0

    lax.fori_loop(0, total_ref[0], step, 0)


def mixed_row(sums, row):
    total = sums[row]
    channels = total.shape[0] // 2
    total = total[:, :BLOCK] + total[:, BLOCK:]
    return total[:channels] + total[channels:]


def mix_in_body(nodes, cols, ids_ref, total_ref, list_ref, row_ref, pack_ref, *refs):
    pieces, outs = refs[:nodes], refs[nodes : nodes + cols]
    values, sums = refs[nodes + cols :]
    rows = sums.shape[0]
    node, col = ids_ref[0], ids_ref[1]
    for offset in range(nodes):
        base = (node ^ offset) * rows
        for part in range(rows):
            store_block(values, base + part, pieces[offset][:, part * BLOCK : (part + 1) * BLOCK])
    mix_rows(total_ref, list_ref, row_ref, pack_ref, values, sums)
    slice_rows = rows // cols
    for offset in range(cols):
        for part in range(slice_rows):
            row = (col ^ offset) * slice_rows + part
            outs[offset][:, part * BLOCK : (part + 1) * BLOCK] = mixed_row(sums, row)


def dense_body(cols, per, ids_ref, *refs):
    pieces, weights = refs[:cols], refs[cols : 2 * cols]
    mixed_ref, hidden_ref, slope_ref, weight_out_ref = refs[2 * cols + 1 : 2 * cols + 5]
    outs = refs[2 * cols + 5 : 3 * cols + 5]
    held, held_weights, scores = refs[-3:]
    col = ids_ref[1]
    for offset in range(cols):
        held[col ^ offset] = pieces[offset][...]
        held_weights[col ^ offset] = weights[offset][...]
    feats = held.shape[1]
    units, classes = weight_out_ref.shape
    mixed = held[...].reshape(mixed_ref.shape)
    mixed_ref[...] = mixed
    weight_in = held_weights[:, :feats].reshape(feats * cols, units)
    own = units // cols
    weight_out = held_weights[:, feats : feats + own].reshape(units, units)[:, :classes]
    weight_out_ref[...] = weight_out
    bias_in = jnp.concatenate(
        [held_weights[group, feats + own : feats + own + 1, :own] for group in range(cols)], axis=1
    )
    inner = product(weight_in, mixed, ((0,), (0,))) + as_column(bias_in)
    bend = jnp.tanh(CURVE * (inner + CUBIC * inner * inner * inner))
    hidden = 0.5 * inner * (1.0 + bend)
    hidden_ref[...] = hidden
    slope_ref[...] = 0.5 * (1.0 + bend) + (0.5 * inner) * (1.0 - bend * bend) * (
        CURVE * (1.0 + 3.0 * CUBIC * inner * inner)
    )
    value = product(weight_out, hidden, ((0,), (0,)))
    scores[...] = jnp.zeros_like(scores)
    for group in range(cols):
        scores[group, :per] = value[group * per : (group + 1) * per]
    for offset in range(cols):
        outs[offset][...] = scores[col ^ offset]


def stack_body(*refs):
    for index, ref in enumerate(refs[:-2]):
        refs[-1][index] = ref[...]


def mix_out_body(nodes, cols, per, ids_ref, total_ref, list_ref, row_ref, pack_ref, bias_ref, labels_ref, *refs):
    pieces = refs[:nodes]
    upper_ref, lower_ref, stats_ref, values, sums, groups = refs[nodes:]
    rows = sums.shape[0]
    node, col = ids_ref[0], ids_ref[1]
    slice_rows = rows // cols
    column = as_column(bias_ref[...])
    groups[...] = jnp.zeros_like(groups)
    for group in range(cols):
        groups[group, :per] = column[group * per : (group + 1) * per]
    for offset in range(nodes):
        base = (node ^ offset) * rows
        for group in range(cols):
            for part in range(slice_rows):
                store_block(
                    values,
                    base + (col ^ group) * slice_rows + part,
                    pieces[offset][group, :, part * BLOCK : (part + 1) * BLOCK],
                )
    mix_rows(total_ref, list_ref, row_ref, pack_ref, values, sums)
    for row in range(rows):
        at = slice(row * BLOCK, (row + 1) * BLOCK)
        total = mixed_row(sums, row) + groups[col]
        upper_ref[:, at] = total[:HALF]
        lower_ref[:, at] = total[HALF:]
    logits = jnp.concatenate([upper_ref[...], lower_ref[...]], axis=0)
    place = lax.broadcasted_iota(jnp.int32, logits.shape, 0)
    inside = place < per
    top = jnp.max(jnp.where(inside, logits, -jnp.inf), axis=0, keepdims=True)
    total = jnp.sum(jnp.where(inside, jnp.exp(logits - top), 0.0), axis=0, keepdims=True)
    hit = inside & (place + col * per == labels_ref[...])
    chosen = jnp.sum(jnp.where(hit, logits, 0.0), axis=0, keepdims=True)
    stats_ref[...] = jnp.zeros_like(stats_ref)
    stats_ref[0:1] = top
    stats_ref[1:2] = total
    stats_ref[2:3] = chosen


def mix_back_body(nodes, cols, per, ids_ref, total_ref, list_ref, row_ref, pack_ref, upper_ref, lower_ref, labels_ref, mask_ref, *refs):
    stats, outs = refs[:cols], refs[cols : cols + nodes]
    extra_ref, sums, grads = refs[cols + nodes :]
    rows = grads.shape[0]
    node, col = ids_ref[0], ids_ref[1]
    tops = [ref[0:1] for ref in stats]
    top = functools.reduce(jnp.maximum, tops)
    total = sum(ref[1:2] * jnp.exp(at - top) for ref, at in zip(stats, tops))
    chosen = sum(ref[2:3] for ref in stats)
    mask = mask_ref[...].astype(f32)
    logits = jnp.concatenate([upper_ref[...], lower_ref[...]], axis=0)
    place = lax.broadcasted_iota(jnp.int32, logits.shape, 0)
    inside = place < per
    hit = place + col * per == labels_ref[...]
    chance = jnp.exp(logits - top) * (1.0 / total)
    grad = jnp.where(inside, mask * (chance - hit.astype(f32)), 0.0)
    high, low = split(grad)
    ones = jnp.ones((8, grad.shape[1]), bf16)
    bias_row = lax.dot_general(
        ones, high, (((1,), (1,)), ((), ())), preferred_element_type=f32
    ) + lax.dot_general(ones, low, (((1,), (1,)), ((), ())), preferred_element_type=f32)
    loss = jnp.sum(mask * (top + jnp.log(total) - chosen), axis=1, keepdims=True)
    number = jnp.sum(mask, axis=1, keepdims=True)
    first = (col == 0).astype(f32)
    extra_ref[...] = jnp.zeros_like(extra_ref)
    line = lax.broadcasted_iota(jnp.int32, bias_row.shape, 0)
    extra_ref[:, : high.shape[0]] = jnp.where(line == col, bias_row, 0.0)
    extra_ref[cols : cols + 1, 0:1] = loss * first
    extra_ref[cols : cols + 1, 1:2] = number * first

    for row in range(rows):
        at = slice(row * BLOCK, (row + 1) * BLOCK)
        grads[row] = jnp.concatenate(
            [
                jnp.concatenate([high[:, at], high[:, at]], axis=1),
                jnp.concatenate([low[:, at], low[:, at]], axis=1),
            ],
            axis=0,
        )
    sums[...] = jnp.zeros_like(sums)

    def step(group, _):
        for part in range(UNROLL):
            item = group * UNROLL + part
            terms = jnp.dot(grads[row_ref[item]], pack_ref[item], preferred_element_type=f32)
            half = terms.shape[0] // 2
            terms = terms[:half] + terms[half:]
            for q in range(CHUNK):
                to = list_ref[item * CHUNK + q]
                sums[to] = sums[to] + terms[:, q * BLOCK : (q + 1) * BLOCK]
        return 0

    lax.fori_loop(0, total_ref[0], step, 0)
    for offset in range(nodes):
        base = (node ^ offset) * rows
        for part in range(rows):
            outs[offset][:, part * BLOCK : (part + 1) * BLOCK] = sums[base + part]


def pair_body(*refs):
    count = len(refs) // 3
    for index in range(count):
        refs[2 * count + index][...] = refs[index][...] + refs[count + index][...]


def sum_body(cols, ids_ref, *refs):
    parts, outs, held = refs[: -cols - 1], refs[-cols - 1 : -1], refs[-1]
    col = ids_ref[1]
    total = sum((ref[...] for ref in parts[1:]), parts[0][...])
    width = total.shape[1] // cols
    for group in range(cols):
        held[group] = total[:, group * width : (group + 1) * width]
    for offset in range(cols):
        outs[offset][...] = held[col ^ offset]


def grads_body(cols, per, ids_ref, mixed_ref, hidden_ref, slope_ref, weight_out_ref, extra_ref, *refs):
    pieces = refs[:cols]
    keep_ref, send_ref, held, packed = refs[cols:]
    core, col = ids_ref[0] & 1, ids_ref[1]
    for offset in range(cols):
        held[col ^ offset] = pieces[offset][...]
    spread = jnp.concatenate([held[group, :per] for group in range(cols)], axis=0)
    classes = spread.shape[0]
    hidden_grad = product(weight_out_ref[...], spread, ((1,), (0,)))
    inner_grad = hidden_grad * slope_ref[...]
    weight_in = product(mixed_ref[...], inner_grad, ((1,), (1,)))
    weight_out = product(hidden_ref[...], spread, ((1,), (1,)))
    bias_in = jnp.sum(inner_grad, axis=1, keepdims=True)
    feats, units = weight_in.shape[0] // cols, weight_out.shape[0] // cols
    packed[...] = jnp.zeros_like(packed)
    for group in range(cols):
        packed[group, :feats] = weight_in[group * feats : (group + 1) * feats]
        rows = slice(group * units, (group + 1) * units)
        packed[group, feats : feats + units, :classes] = weight_out[rows]
        packed[group, feats : feats + units, classes : classes + 1] = bias_in[rows]
        packed[group, feats + units : feats + units + 8] = extra_ref[...]
    half = packed.shape[1] // 2
    for offset in range(cols):
        keep_ref[offset] = packed[col ^ offset, pl.ds(pl.multiple_of(core * half, 8), half)]
        send_ref[offset] = packed[col ^ offset, pl.ds(pl.multiple_of((1 - core) * half, 8), half)]


def finish_body(cols, per, ids_ref, mine_ref, other_ref, weight_in_ref, bias_in_ref, weight_out_ref, bias_out_ref, loss_ref, whole):
    core = ids_ref[0] & 1
    half = mine_ref.shape[0]
    whole[core] = mine_ref[...]
    whole[1 - core] = other_ref[...]
    value = whole[...].reshape(2 * half, mine_ref.shape[1])
    feats, (units, classes) = weight_in_ref.shape[0], weight_out_ref.shape
    weight_in_ref[...] = value[:feats]
    weight_out_ref[...] = value[feats : feats + units, :classes]
    bias_in_ref[...] = as_row(value[feats : feats + units, classes : classes + 1])
    extra = value[feats + units : feats + units + 8]
    bias_out_ref[...] = jnp.concatenate([extra[group : group + 1, :per] for group in range(cols)], axis=1)
    loss_ref[...] = extra[cols : cols + 1, 0:1] / jnp.maximum(extra[cols : cols + 1, 1:2], 1.0)


def logits_body(cols, per, ids_ref, *refs):
    uppers, lowers, out_ref, held = refs[:cols], refs[cols : 2 * cols], refs[-2], refs[-1]
    col = ids_ref[1]
    for offset in range(cols):
        held[col ^ offset, :HALF] = uppers[offset][...]
        held[col ^ offset, HALF:] = lowers[offset][...]
    out_ref[...] = jnp.concatenate([held[group, :per] for group in range(cols)], axis=0)


def gather_chips(value, nodes):
    return [value] + [exchange(value, "node", offset) for offset in range(2, nodes, 2)]


def gather_cores(even):
    odd = [exchange(piece, "node", 1) for piece in even]
    return [piece for pair in zip(even, odd) for piece in pair]


def on_device(
    features,
    tiles,
    tile_column,
    tile_count,
    labels,
    train_mask,
    weight_in,
    bias_in,
    weight_out,
    bias_out,
):
    nodes, cols = lax.axis_size("node"), lax.axis_size("col")
    rows = tile_column.shape[0]
    local = labels.shape[0]
    slice_nodes = local // cols
    block_total = nodes * rows
    feats = features.shape[0]
    classes = weight_out.shape[1]
    per = classes // cols
    units = weight_out.shape[0] * cols
    shape = jax.ShapeDtypeStruct
    ids = jnp.stack([lax.axis_index("node"), lax.axis_index("col")]).astype(jnp.int32)

    labels = labels[None, :]
    train_mask = train_mask[None, :]
    own = units // cols
    height = feats + own + 8
    weights = (
        jnp.pad(weight_in, ((0, height - feats), (0, 0)))
        + jnp.pad(weight_out, ((feats, 8), (0, units - classes)))
        + jnp.pad(bias_in[None, :], ((feats + own, 7), (0, units - own)))
    )
    ids, tile_count = lax.optimization_barrier((ids, tile_count))
    even = gather_chips(features, nodes)
    weight_pieces = [weights] + [exchange(weights, "col", k) for k in range(1, cols)]
    packed, listed, placed, steps = pack(tiles, tile_column, tile_count, block_total)
    steps, even, weight_pieces = lax.optimization_barrier((steps, even, weight_pieces))
    feature_pieces = gather_cores(even)
    packed = pltpu.with_memory_space_constraint(packed, pltpu.VMEM)
    sparse = (ids, steps, listed, placed, packed)
    sparse_specs = [SMEM] * 4 + [VMEM]

    mixed_parts = call(
        functools.partial(mix_in_body, nodes, cols),
        [shape((feats, slice_nodes), f32)] * cols,
        [pltpu.VMEM((block_total, 2 * feats, BLOCK), bf16), pltpu.VMEM((rows, 2 * feats, 2 * BLOCK), f32)],
        *sparse,
        *feature_pieces,
        specs=sparse_specs + [VMEM] * nodes,
        limit=20,
        flops=10**9,
        moved=16 * MIB,
    )
    mixed_pieces = [mixed_parts[0]] + [exchange(mixed_parts[k], "col", k) for k in range(1, cols)]
    mixed, hidden, slope, weight_out_all, *score_parts = call(
        functools.partial(dense_body, cols, per),
        [shape((feats * cols, slice_nodes), f32)]
        + [shape((units, slice_nodes), f32)] * 2
        + [shape((units, classes), f32)]
        + [shape((PAD, slice_nodes), f32)] * cols,
        [
            pltpu.VMEM((cols, feats, slice_nodes), f32),
            pltpu.VMEM((cols, *weights.shape), f32),
            pltpu.VMEM((cols, PAD, slice_nodes), f32),
        ],
        ids,
        *mixed_pieces,
        *weight_pieces,
        packed,
        specs=[SMEM] + [VMEM] * (2 * cols + 1),
        flops=10**8,
        moved=2 * MIB,
    )
    score_pieces = [score_parts[0]] + [exchange(score_parts[k], "col", k) for k in range(1, cols)]
    (stacked,) = call(
        stack_body,
        [shape((cols, PAD, slice_nodes), f32)],
        [],
        *score_pieces, packed,
        limit=20,
        moved=MIB,
    )
    scores = gather_cores(gather_chips(stacked, nodes))
    upper, lower, stats = call(
        functools.partial(mix_out_body, nodes, cols, per),
        [shape((HALF, local), f32), shape((PAD - HALF, local), f32), shape((8, local), f32)],
        [pltpu.VMEM((block_total, 2 * PAD, BLOCK), bf16), pltpu.VMEM((rows, 2 * PAD, 2 * BLOCK), f32), pltpu.VMEM((cols, PAD, 1), f32)],
        *sparse,
        bias_out[None, :],
        labels,
        *scores,
        specs=sparse_specs + [VMEM] * (2 + nodes),
        limit=20,
        flops=10**9,
        moved=16 * MIB,
    )
    stats_pieces = [stats] + [exchange(stats, "col", k) for k in range(1, cols)]
    *spread_parts, extra = call(
        functools.partial(mix_back_body, nodes, cols, per),
        [shape((PAD, local), f32)] * nodes + [shape((8, 2 * BLOCK), f32)],
        [
            pltpu.VMEM((block_total, PAD, BLOCK), f32),
            pltpu.VMEM((rows, 2 * PAD, 2 * BLOCK), bf16),
        ],
        *sparse,
        upper,
        lower,
        labels,
        train_mask,
        *stats_pieces,
        specs=sparse_specs + [VMEM] * (4 + cols),
        limit=20,
        flops=10**9,
        moved=16 * MIB,
    )
    uppers = [upper] + [exchange(upper, "col", k) for k in range(1, cols)]
    spread_parts, uppers = lax.optimization_barrier((spread_parts, uppers))
    paired = call(
        pair_body,
        [shape((PAD, local), f32)] * (nodes // 2),
        [],
        *spread_parts[::2],
        *[exchange(part, "node", 1) for part in spread_parts[1::2]],
        limit=20,
        moved=2 * MIB,
    )
    paired, lower = lax.optimization_barrier((paired, lower))
    chips = [exchange(paired[k], "node", 2 * k) for k in range(1, nodes // 2)]
    lowers = [lower] + [exchange(lower, "col", k) for k in range(1, cols)]
    spread_slices = call(
        functools.partial(sum_body, cols),
        [shape((PAD, slice_nodes), f32)] * cols,
        [pltpu.VMEM((cols, PAD, slice_nodes), f32)],
        ids,
        paired[0],
        *chips,
        specs=[SMEM] + [VMEM] * (nodes // 2),
        limit=20,
        moved=MIB,
    )
    spread_slices, lowers = lax.optimization_barrier((spread_slices, lowers))
    spread_pieces = [spread_slices[0]] + [exchange(spread_slices[k], "col", k) for k in range(1, cols)]
    (logits,) = call(
        functools.partial(logits_body, cols, per),
        [shape((classes, local), f32)],
        [pltpu.VMEM((cols, PAD, local), f32)],
        ids,
        *uppers,
        *lowers,
        specs=[SMEM] + [VMEM] * (2 * cols),
        limit=20,
        moved=2 * MIB,
    )
    logits, *spread_pieces = lax.optimization_barrier((logits, *spread_pieces))

    height = -(-(feats + units // cols + 8) // 16) * 16
    keep, send = call(
        functools.partial(grads_body, cols, per),
        [shape((cols, height // 2, units), f32)] * 2,
        [pltpu.VMEM((cols, PAD, slice_nodes), f32), pltpu.VMEM((cols, height, units), f32)],
        ids,
        mixed,
        hidden,
        slope,
        weight_out_all,
        extra,
        *spread_pieces,
        specs=[SMEM] + [VMEM] * (5 + cols),
        flops=10**8,
        moved=2 * MIB,
    )
    halves = keep + exchange(send, "node", 1)
    total = halves[0]
    for k in range(1, cols):
        total = total + exchange(halves[k], "col", k)
    grand = total
    for k in range(2, nodes, 2):
        grand = grand + exchange(total, "node", k)
    other = exchange(grand, "node", 1)
    grad_in, grad_bias_in, grad_out, grad_bias_out, mean_loss = call(
        functools.partial(finish_body, cols, per),
        [
            shape((feats, units), f32),
            shape((1, units // cols), f32),
            shape((units // cols, classes), f32),
            shape((1, classes), f32),
            shape((1, 1), f32),
        ],
        [pltpu.VMEM((2, height // 2, units), f32)],
        ids,
        grand,
        other,
        specs=[SMEM, VMEM, VMEM],
    )
    return (
        logits,
        mean_loss.reshape(()),
        grad_in,
        grad_bias_in.reshape(-1),
        grad_out,
        grad_bias_out.reshape(-1),
    )


def solution(mesh):
    in_specs = (
        P("col", "node"),
        P("node", None, None, None),
        P("node", None),
        P("node"),
        P("node"),
        P("node"),
        P("col", None),
        P("col"),
        P("col", None),
        P(),
    )
    out_specs = (P(None, "node"), P(), P("col", None), P("col"), P("col", None), P())
    return jax.shard_map(
        on_device, mesh=mesh, in_specs=in_specs, out_specs=out_specs, check_vma=False
    )
```

```python
import functools

import jax
import jax.numpy as jnp
from jax import lax
from jax.experimental import pallas as pl
from jax.experimental.pallas import tpu as pltpu
from jax.sharding import PartitionSpec as P

BLOCK = 128
CHUNK = 4
UNROLL = 8
DEPTH = 3
PAD = 48
HALF = 24

f32 = jnp.float32
bf16 = jnp.bfloat16
VMEM = pl.BlockSpec(memory_space=pltpu.VMEM)
SMEM = pl.BlockSpec(memory_space=pltpu.SMEM)
MIB = 1 << 20

CURVE = 0.7978845608028654
CUBIC = 0.044715


def exchange(value, axis, offset):
    total = lax.axis_size(axis)
    return lax.ppermute(value, axis, [(i, i ^ offset) for i in range(total)])


def split(value):
    high = value.astype(bf16)
    low = (value - high.astype(f32)).astype(bf16)
    return high, low


def product(left, right, dims):
    lh, ll = split(left)
    rh, rl = split(right)

    def one(a, b):
        return lax.dot_general(a, b, (dims, ((), ())), preferred_element_type=f32)

    return one(lh, rh) + (one(lh, rl) + one(ll, rh))


def call(body, outs, scratch, *args, specs=None, out_specs=None, limit=20, flops=0, moved=0):
    return pl.pallas_call(
        body,
        out_shape=outs,
        in_specs=specs or [VMEM] * len(args),
        out_specs=out_specs or [VMEM] * len(outs),
        scratch_shapes=scratch,
        compiler_params=pltpu.CompilerParams(vmem_limit_bytes=limit * MIB),
        cost_estimate=pl.CostEstimate(flops=flops, bytes_accessed=moved, transcendentals=0),
    )(*args)


def as_column(row):
    size = row.shape[1]
    shape = (size, size)
    same = lax.broadcasted_iota(jnp.int32, shape, 0) == lax.broadcasted_iota(jnp.int32, shape, 1)
    return jnp.sum(jnp.where(same, row, 0.0), axis=1, keepdims=True)


def as_row(column):
    size = column.shape[0]
    shape = (size, size)
    same = lax.broadcasted_iota(jnp.int32, shape, 0) == lax.broadcasted_iota(jnp.int32, shape, 1)
    return jnp.sum(jnp.where(same, column, 0.0), axis=0, keepdims=True)


def pack_body(
    count_in, column_in, tiles_ref, pack_ref, list_ref, row_ref, total_ref,
    count_ref, column_ref, land, place, owner, twin_from, twin_to, sem, list_sem,
):
    rows, slots = column_ref.shape
    lists = [
        pltpu.make_async_copy(count_in, count_ref, list_sem.at[0]),
        pltpu.make_async_copy(column_in, column_ref, list_sem.at[1]),
    ]
    for copy in lists:
        copy.start()
    for copy in lists:
        copy.wait()

    def copies(row, act):
        ring = lax.rem(row, DEPTH)
        live = count_ref[row]
        for power in range(slots.bit_length()):
            size = 1 << power

            @pl.when(live & size != 0)
            def _():
                first = live & ~(2 * size - 1)
                act(
                    pltpu.make_async_copy(
                        tiles_ref.at[row, pl.ds(first, size)],
                        land.at[pl.ds(ring * slots + first, size)],
                        sem.at[ring, power],
                    )
                )

    def start(copy):
        copy.start()

    def wait(copy):
        copy.wait()

    for row in range(DEPTH):
        copies(row, start)
    land[DEPTH * slots] = jnp.zeros((BLOCK, BLOCK), f32)

    def clear(index, _):
        place[index] = -1
        return 0

    lax.fori_loop(0, place.shape[0], clear, 0)

    def one_row(row, begin):
        stamp = row * slots
        shift = stamp - lax.rem(row, DEPTH) * slots

        def scan(slot, state):
            found, twins = state
            column = column_ref[row, slot]
            at = place[column]
            fresh = at < stamp
            place[column] = jnp.where(fresh, stamp + slot, at)
            owner[found] = stamp - shift + slot
            list_ref[begin * CHUNK + found] = column
            twin_from[twins] = stamp - shift + slot
            twin_to[twins] = at - shift
            step = fresh.astype(jnp.int32)
            return found + step, twins + 1 - step

        found, twins = lax.fori_loop(0, count_ref[row], scan, (0, 0))
        steps = (found + CHUNK - 1) // CHUNK

        def blank(index, _):
            list_ref[begin * CHUNK + index] = 0
            owner[index] = DEPTH * slots
            return 0

        lax.fori_loop(found, steps * CHUNK, blank, 0)
        copies(row, wait)

        def join(index, _):
            to = twin_to[index]
            land[to] = land[to] + land[twin_from[index]]
            return 0

        lax.fori_loop(0, twins, join, 0)

        def convert(step, _):
            item = begin + step
            row_ref[item] = row
            for q in range(CHUNK):
                at = slice(q * BLOCK, (q + 1) * BLOCK)
                high, low = split(land[owner[step * CHUNK + q]])
                pack_ref[item, :BLOCK, at] = high
                pack_ref[item, BLOCK:, at] = low
            return 0

        lax.fori_loop(0, steps, convert, 0)

        @pl.when(row + DEPTH < rows)
        def _():
            copies(row + DEPTH, start)

        return begin + steps

    used = lax.fori_loop(0, rows, one_row, 0)
    total = (used + UNROLL - 1) // UNROLL * UNROLL

    def fill(item, _):
        row_ref[item] = 0
        for q in range(CHUNK):
            list_ref[item * CHUNK + q] = 0
        pack_ref[item] = jnp.zeros(pack_ref.shape[1:], bf16)
        return 0

    lax.fori_loop(used, total, fill, 0)
    total_ref[0] = total // UNROLL


def pack(tiles, tile_column, tile_count, block_total):
    rows, slots = tile_column.shape
    items = -(-rows * slots // (CHUNK * UNROLL)) * UNROLL
    shape = jax.ShapeDtypeStruct
    return call(
        pack_body,
        [
            pltpu.VMEM((items, 2 * BLOCK, CHUNK * BLOCK), bf16),
            shape((items * CHUNK,), jnp.int32),
            shape((items,), jnp.int32),
            shape((1,), jnp.int32),
        ],
        [
            pltpu.SMEM(tile_count.shape, jnp.int32),
            pltpu.SMEM(tile_column.shape, jnp.int32),
            pltpu.VMEM((DEPTH * slots + 1, BLOCK, BLOCK), f32),
            pltpu.SMEM((block_total,), jnp.int32),
            pltpu.SMEM((slots,), jnp.int32),
            pltpu.SMEM((slots,), jnp.int32),
            pltpu.SMEM((slots,), jnp.int32),
            pltpu.SemaphoreType.DMA((DEPTH, slots.bit_length())),
            pltpu.SemaphoreType.DMA((2,)),
        ],
        pltpu.with_memory_space_constraint(tile_count, pltpu.HBM),
        pltpu.with_memory_space_constraint(tile_column, pltpu.HBM),
        tiles,
        specs=[pl.BlockSpec(memory_space=pl.ANY)] * 3,
        out_specs=[VMEM, SMEM, SMEM, SMEM],
        limit=20,
        flops=10**8,
        moved=40 * MIB,
    )


def bring(total_ref, pack_ref, store, sem):
    def one(group):
        part = pl.ds(group * UNROLL, UNROLL)
        return pltpu.make_async_copy(pack_ref.at[part], store.at[part], sem.at[group])

    def start(group, _):
        one(group).start()
        return 0

    lax.fori_loop(0, total_ref[0], start, 0)
    return one


def store_block(values, at, value):
    channels = value.shape[0]
    high, low = split(value)
    values[at, :channels] = high
    values[at, channels:] = low


def mix_rows(total_ref, list_ref, row_ref, store, values, sums):
    sums[...] = jnp.zeros_like(sums)

    def step(group, _):
        for part in range(UNROLL):
            item = group * UNROLL + part
            left = jnp.concatenate([values[list_ref[item * CHUNK + q]] for q in range(CHUNK)], axis=1)
            row = row_ref[item]
            sums[row] = sums[row] + lax.dot_general(
                left, store[item], (((1,), (1,)), ((), ())), preferred_element_type=f32
            )
        return 0

    lax.fori_loop(0, total_ref[0], step, 0)


def mixed_row(sums, row):
    total = sums[row]
    channels = total.shape[0] // 2
    total = total[:, :BLOCK] + total[:, BLOCK:]
    return total[:channels] + total[channels:]


def mix_in_body(nodes, cols, ids_ref, total_ref, list_ref, row_ref, pack_ref, *refs):
    pieces, outs = refs[:nodes], refs[nodes : nodes + cols]
    values, sums = refs[nodes + cols :]
    rows = sums.shape[0]
    node, col = ids_ref[0], ids_ref[1]
    for offset in range(nodes):
        base = (node ^ offset) * rows
        for part in range(rows):
            store_block(values, base + part, pieces[offset][:, part * BLOCK : (part + 1) * BLOCK])
    mix_rows(total_ref, list_ref, row_ref, pack_ref, values, sums)
    slice_rows = rows // cols
    for offset in range(cols):
        for part in range(slice_rows):
            row = (col ^ offset) * slice_rows + part
            outs[offset][:, part * BLOCK : (part + 1) * BLOCK] = mixed_row(sums, row)


def dense_body(cols, per, ids_ref, *refs):
    pieces, weights = refs[:cols], refs[cols : 2 * cols]
    mixed_ref, hidden_ref, slope_ref, weight_out_ref = refs[2 * cols + 1 : 2 * cols + 5]
    outs = refs[2 * cols + 5 : 3 * cols + 5]
    held, held_weights, scores = refs[-3:]
    col = ids_ref[1]
    for offset in range(cols):
        held[col ^ offset] = pieces[offset][...]
        held_weights[col ^ offset] = weights[offset][...]
    feats = held.shape[1]
    units, classes = weight_out_ref.shape
    mixed = held[...].reshape(mixed_ref.shape)
    mixed_ref[...] = mixed
    weight_in = held_weights[:, :feats].reshape(feats * cols, units)
    own = units // cols
    weight_out = held_weights[:, feats : feats + own].reshape(units, units)[:, :classes]
    weight_out_ref[...] = weight_out
    bias_in = jnp.concatenate(
        [held_weights[group, feats + own : feats + own + 1, :own] for group in range(cols)], axis=1
    )
    inner = product(weight_in, mixed, ((0,), (0,))) + as_column(bias_in)
    bend = jnp.tanh(CURVE * (inner + CUBIC * inner * inner * inner))
    hidden = 0.5 * inner * (1.0 + bend)
    hidden_ref[...] = hidden
    slope_ref[...] = 0.5 * (1.0 + bend) + (0.5 * inner) * (1.0 - bend * bend) * (
        CURVE * (1.0 + 3.0 * CUBIC * inner * inner)
    )
    value = product(weight_out, hidden, ((0,), (0,)))
    scores[...] = jnp.zeros_like(scores)
    for group in range(cols):
        scores[group, :per] = value[group * per : (group + 1) * per]
    for offset in range(cols):
        outs[offset][...] = scores[col ^ offset]


def stack_body(*refs):
    for index, ref in enumerate(refs[:-2]):
        refs[-1][index] = ref[...]


def mix_out_body(nodes, cols, per, ids_ref, total_ref, list_ref, row_ref, pack_ref, bias_ref, labels_ref, *refs):
    pieces = refs[:nodes]
    upper_ref, lower_ref, stats_ref, values, sums, groups = refs[nodes:]
    rows = sums.shape[0]
    node, col = ids_ref[0], ids_ref[1]
    slice_rows = rows // cols
    column = as_column(bias_ref[...])
    groups[...] = jnp.zeros_like(groups)
    for group in range(cols):
        groups[group, :per] = column[group * per : (group + 1) * per]
    for offset in range(nodes):
        base = (node ^ offset) * rows
        for group in range(cols):
            for part in range(slice_rows):
                store_block(
                    values,
                    base + (col ^ group) * slice_rows + part,
                    pieces[offset][group, :, part * BLOCK : (part + 1) * BLOCK],
                )
    mix_rows(total_ref, list_ref, row_ref, pack_ref, values, sums)
    for row in range(rows):
        at = slice(row * BLOCK, (row + 1) * BLOCK)
        total = mixed_row(sums, row) + groups[col]
        upper_ref[:, at] = total[:HALF]
        lower_ref[:, at] = total[HALF:]
    logits = jnp.concatenate([upper_ref[...], lower_ref[...]], axis=0)
    place = lax.broadcasted_iota(jnp.int32, logits.shape, 0)
    inside = place < per
    top = jnp.max(jnp.where(inside, logits, -jnp.inf), axis=0, keepdims=True)
    total = jnp.sum(jnp.where(inside, jnp.exp(logits - top), 0.0), axis=0, keepdims=True)
    hit = inside & (place + col * per == labels_ref[...])
    chosen = jnp.sum(jnp.where(hit, logits, 0.0), axis=0, keepdims=True)
    stats_ref[...] = jnp.zeros_like(stats_ref)
    stats_ref[0:1] = top
    stats_ref[1:2] = total
    stats_ref[2:3] = chosen


def mix_back_body(nodes, cols, per, ids_ref, total_ref, list_ref, row_ref, pack_ref, upper_ref, lower_ref, labels_ref, mask_ref, *refs):
    stats, outs = refs[:cols], refs[cols : cols + nodes]
    extra_ref, sums, grads = refs[cols + nodes :]
    rows = grads.shape[0]
    node, col = ids_ref[0], ids_ref[1]
    tops = [ref[0:1] for ref in stats]
    top = functools.reduce(jnp.maximum, tops)
    total = sum(ref[1:2] * jnp.exp(at - top) for ref, at in zip(stats, tops))
    chosen = sum(ref[2:3] for ref in stats)
    mask = mask_ref[...].astype(f32)
    logits = jnp.concatenate([upper_ref[...], lower_ref[...]], axis=0)
    place = lax.broadcasted_iota(jnp.int32, logits.shape, 0)
    inside = place < per
    hit = place + col * per == labels_ref[...]
    chance = jnp.exp(logits - top) * (1.0 / total)
    grad = jnp.where(inside, mask * (chance - hit.astype(f32)), 0.0)
    high, low = split(grad)
    ones = jnp.ones((8, grad.shape[1]), bf16)
    bias_row = lax.dot_general(
        ones, high, (((1,), (1,)), ((), ())), preferred_element_type=f32
    ) + lax.dot_general(ones, low, (((1,), (1,)), ((), ())), preferred_element_type=f32)
    loss = jnp.sum(mask * (top + jnp.log(total) - chosen), axis=1, keepdims=True)
    number = jnp.sum(mask, axis=1, keepdims=True)
    first = (col == 0).astype(f32)
    extra_ref[...] = jnp.zeros_like(extra_ref)
    line = lax.broadcasted_iota(jnp.int32, bias_row.shape, 0)
    extra_ref[:, : high.shape[0]] = jnp.where(line == col, bias_row, 0.0)
    extra_ref[cols : cols + 1, 0:1] = loss * first
    extra_ref[cols : cols + 1, 1:2] = number * first

    for row in range(rows):
        at = slice(row * BLOCK, (row + 1) * BLOCK)
        grads[row] = jnp.concatenate(
            [
                jnp.concatenate([high[:, at], high[:, at]], axis=1),
                jnp.concatenate([low[:, at], low[:, at]], axis=1),
            ],
            axis=0,
        )
    sums[...] = jnp.zeros_like(sums)

    def step(group, _):
        for part in range(UNROLL):
            item = group * UNROLL + part
            terms = jnp.dot(grads[row_ref[item]], pack_ref[item], preferred_element_type=f32)
            half = terms.shape[0] // 2
            terms = terms[:half] + terms[half:]
            for q in range(CHUNK):
                to = list_ref[item * CHUNK + q]
                sums[to] = sums[to] + terms[:, q * BLOCK : (q + 1) * BLOCK]
        return 0

    lax.fori_loop(0, total_ref[0], step, 0)
    for offset in range(nodes):
        base = (node ^ offset) * rows
        for part in range(rows):
            outs[offset][:, part * BLOCK : (part + 1) * BLOCK] = sums[base + part]


def pair_body(*refs):
    count = len(refs) // 3
    for index in range(count):
        refs[2 * count + index][...] = refs[index][...] + refs[count + index][...]


def sum_body(cols, ids_ref, *refs):
    parts, outs, held = refs[: -cols - 1], refs[-cols - 1 : -1], refs[-1]
    col = ids_ref[1]
    total = sum((ref[...] for ref in parts[1:]), parts[0][...])
    width = total.shape[1] // cols
    for group in range(cols):
        held[group] = total[:, group * width : (group + 1) * width]
    for offset in range(cols):
        outs[offset][...] = held[col ^ offset]


def grads_body(cols, per, ids_ref, mixed_ref, hidden_ref, slope_ref, weight_out_ref, extra_ref, *refs):
    pieces = refs[:cols]
    keep_ref, send_ref, held, packed = refs[cols:]
    core, col = ids_ref[0] & 1, ids_ref[1]
    for offset in range(cols):
        held[col ^ offset] = pieces[offset][...]
    spread = jnp.concatenate([held[group, :per] for group in range(cols)], axis=0)
    hidden_grad = product(weight_out_ref[...], spread, ((1,), (0,)))
    inner_grad = hidden_grad * slope_ref[...]
    weight_in = product(mixed_ref[...], inner_grad, ((1,), (1,)))
    weight_out = product(spread, hidden_ref[...], ((1,), (1,)))
    bias_in = as_row(jnp.sum(inner_grad, axis=1, keepdims=True))
    feats, units = weight_in.shape[0] // cols, weight_out.shape[1] // cols
    extra = extra_ref[: cols + 1]
    line = lax.broadcasted_iota(jnp.int32, extra.shape, 0)
    for group in range(cols):
        mine = slice(group * units, (group + 1) * units)
        folded = jnp.concatenate([weight_out[q * per : (q + 1) * per, mine] for q in range(cols)], axis=1)
        spare = jnp.zeros((1, BLOCK), f32)
        bias = jnp.concatenate([spare, bias_in[:, mine], spare[:, : BLOCK - units]], axis=1)
        packed[group] = jnp.concatenate(
            [weight_in[group * feats : (group + 1) * feats], folded, jnp.where(line == cols, extra + bias, extra)],
            axis=0,
        )
    half = packed.shape[1] // 2
    for offset in range(cols):
        keep_ref[offset] = packed[col ^ offset, pl.ds(pl.multiple_of(core * half, 8), half)]
        send_ref[offset] = packed[col ^ offset, pl.ds(pl.multiple_of((1 - core) * half, 8), half)]


def finish_body(cols, per, ids_ref, mine_ref, other_ref, weight_in_ref, bias_in_ref, weight_out_ref, bias_out_ref, loss_ref, whole):
    core = ids_ref[0] & 1
    half = mine_ref.shape[0]
    whole[core] = mine_ref[...]
    whole[1 - core] = other_ref[...]
    value = whole[...].reshape(2 * half, mine_ref.shape[1])
    feats, (units, classes) = weight_in_ref.shape[0], weight_out_ref.shape
    weight_in_ref[...] = value[:feats]
    folded = value[feats : feats + per]
    spread = jnp.concatenate([folded[:, q * units : (q + 1) * units] for q in range(cols)], axis=0)
    weight_out_ref[...] = spread.T
    extra = value[feats + per : feats + per + cols + 1]
    bias_in_ref[...] = extra[cols : cols + 1, BLOCK : BLOCK + units]
    bias_out_ref[...] = jnp.concatenate([extra[group : group + 1, :per] for group in range(cols)], axis=1)
    loss_ref[...] = extra[cols : cols + 1, 0:1] / jnp.maximum(extra[cols : cols + 1, 1:2], 1.0)


def logits_body(cols, per, ids_ref, *refs):
    uppers, lowers, out_ref, held = refs[:cols], refs[cols : 2 * cols], refs[-2], refs[-1]
    col = ids_ref[1]
    for offset in range(cols):
        held[col ^ offset, :HALF] = uppers[offset][...]
        held[col ^ offset, HALF:] = lowers[offset][...]
    out_ref[...] = jnp.concatenate([held[group, :per] for group in range(cols)], axis=0)


def gather_chips(value, nodes):
    return [value] + [exchange(value, "node", offset) for offset in range(2, nodes, 2)]


def gather_cores(even):
    odd = [exchange(piece, "node", 1) for piece in even]
    return [piece for pair in zip(even, odd) for piece in pair]


def on_device(
    features,
    tiles,
    tile_column,
    tile_count,
    labels,
    train_mask,
    weight_in,
    bias_in,
    weight_out,
    bias_out,
):
    nodes, cols = lax.axis_size("node"), lax.axis_size("col")
    rows = tile_column.shape[0]
    local = labels.shape[0]
    slice_nodes = local // cols
    block_total = nodes * rows
    feats = features.shape[0]
    classes = weight_out.shape[1]
    per = classes // cols
    units = weight_out.shape[0] * cols
    shape = jax.ShapeDtypeStruct
    ids = jnp.stack([lax.axis_index("node"), lax.axis_index("col")]).astype(jnp.int32)

    labels = labels[None, :]
    train_mask = train_mask[None, :]
    own = units // cols
    height = feats + own + 8
    weights = (
        jnp.pad(weight_in, ((0, height - feats), (0, 0)))
        + jnp.pad(weight_out, ((feats, 8), (0, units - classes)))
        + jnp.pad(bias_in[None, :], ((feats + own, 7), (0, units - own)))
    )
    ids, tile_count = lax.optimization_barrier((ids, tile_count))
    even = gather_chips(features, nodes)
    weight_pieces = [weights] + [exchange(weights, "col", k) for k in range(1, cols)]
    packed, listed, placed, steps = pack(tiles, tile_column, tile_count, block_total)
    steps, even, weight_pieces = lax.optimization_barrier((steps, even, weight_pieces))
    feature_pieces = gather_cores(even)
    packed = pltpu.with_memory_space_constraint(packed, pltpu.VMEM)
    sparse = (ids, steps, listed, placed, packed)
    sparse_specs = [SMEM] * 4 + [VMEM]

    mixed_parts = call(
        functools.partial(mix_in_body, nodes, cols),
        [shape((feats, slice_nodes), f32)] * cols,
        [pltpu.VMEM((block_total, 2 * feats, BLOCK), bf16), pltpu.VMEM((rows, 2 * feats, 2 * BLOCK), f32)],
        *sparse,
        *feature_pieces,
        specs=sparse_specs + [VMEM] * nodes,
        limit=20,
        flops=10**9,
        moved=16 * MIB,
    )
    mixed_pieces = [mixed_parts[0]] + [exchange(mixed_parts[k], "col", k) for k in range(1, cols)]
    mixed, hidden, slope, weight_out_all, *score_parts = call(
        functools.partial(dense_body, cols, per),
        [shape((feats * cols, slice_nodes), f32)]
        + [shape((units, slice_nodes), f32)] * 2
        + [shape((units, classes), f32)]
        + [shape((PAD, slice_nodes), f32)] * cols,
        [
            pltpu.VMEM((cols, feats, slice_nodes), f32),
            pltpu.VMEM((cols, *weights.shape), f32),
            pltpu.VMEM((cols, PAD, slice_nodes), f32),
        ],
        ids,
        *mixed_pieces,
        *weight_pieces,
        packed,
        specs=[SMEM] + [VMEM] * (2 * cols + 1),
        flops=10**8,
        moved=2 * MIB,
    )
    score_pieces = [score_parts[0]] + [exchange(score_parts[k], "col", k) for k in range(1, cols)]
    (stacked,) = call(
        stack_body,
        [shape((cols, PAD, slice_nodes), f32)],
        [],
        *score_pieces, packed,
        limit=20,
        moved=MIB,
    )
    scores = gather_cores(gather_chips(stacked, nodes))
    upper, lower, stats = call(
        functools.partial(mix_out_body, nodes, cols, per),
        [shape((HALF, local), f32), shape((PAD - HALF, local), f32), shape((8, local), f32)],
        [pltpu.VMEM((block_total, 2 * PAD, BLOCK), bf16), pltpu.VMEM((rows, 2 * PAD, 2 * BLOCK), f32), pltpu.VMEM((cols, PAD, 1), f32)],
        *sparse,
        bias_out[None, :],
        labels,
        *scores,
        specs=sparse_specs + [VMEM] * (2 + nodes),
        limit=20,
        flops=10**9,
        moved=16 * MIB,
    )
    stats_pieces = [stats] + [exchange(stats, "col", k) for k in range(1, cols)]
    *spread_parts, extra = call(
        functools.partial(mix_back_body, nodes, cols, per),
        [shape((PAD, local), f32)] * nodes + [shape((8, 2 * BLOCK), f32)],
        [
            pltpu.VMEM((block_total, PAD, BLOCK), f32),
            pltpu.VMEM((rows, 2 * PAD, 2 * BLOCK), bf16),
        ],
        *sparse,
        upper,
        lower,
        labels,
        train_mask,
        *stats_pieces,
        specs=sparse_specs + [VMEM] * (4 + cols),
        limit=20,
        flops=10**9,
        moved=16 * MIB,
    )
    uppers = [upper] + [exchange(upper, "col", k) for k in range(1, cols)]
    spread_parts, uppers = lax.optimization_barrier((spread_parts, uppers))
    paired = call(
        pair_body,
        [shape((PAD, local), f32)] * (nodes // 2),
        [],
        *spread_parts[::2],
        *[exchange(part, "node", 1) for part in spread_parts[1::2]],
        limit=20,
        moved=2 * MIB,
    )
    paired, lower = lax.optimization_barrier((paired, lower))
    chips = [exchange(paired[k], "node", 2 * k) for k in range(1, nodes // 2)]
    lowers = [lower] + [exchange(lower, "col", k) for k in range(1, cols)]
    spread_slices = call(
        functools.partial(sum_body, cols),
        [shape((PAD, slice_nodes), f32)] * cols,
        [pltpu.VMEM((cols, PAD, slice_nodes), f32)],
        ids,
        paired[0],
        *chips,
        specs=[SMEM] + [VMEM] * (nodes // 2),
        limit=20,
        moved=MIB,
    )
    spread_slices, lowers = lax.optimization_barrier((spread_slices, lowers))
    spread_pieces = [spread_slices[0]] + [exchange(spread_slices[k], "col", k) for k in range(1, cols)]
    (logits,) = call(
        functools.partial(logits_body, cols, per),
        [shape((classes, local), f32)],
        [pltpu.VMEM((cols, PAD, local), f32)],
        ids,
        *uppers,
        *lowers,
        specs=[SMEM] + [VMEM] * (2 * cols),
        limit=20,
        moved=2 * MIB,
    )
    logits, *spread_pieces = lax.optimization_barrier((logits, *spread_pieces))

    height = feats + per + cols + 1
    keep, send = call(
        functools.partial(grads_body, cols, per),
        [shape((cols, height // 2, units), f32)] * 2,
        [pltpu.VMEM((cols, PAD, slice_nodes), f32), pltpu.VMEM((cols, height, units), f32)],
        ids,
        mixed,
        hidden,
        slope,
        weight_out_all,
        extra,
        *spread_pieces,
        specs=[SMEM] + [VMEM] * (5 + cols),
        flops=10**8,
        moved=2 * MIB,
    )
    halves = keep + exchange(send, "node", 1)
    total = halves[0]
    for k in range(1, cols):
        total = total + exchange(halves[k], "col", k)
    grand = total
    for k in range(2, nodes, 2):
        grand = grand + exchange(total, "node", k)
    other = exchange(grand, "node", 1)
    grad_in, grad_bias_in, grad_out, grad_bias_out, mean_loss = call(
        functools.partial(finish_body, cols, per),
        [
            shape((feats, units), f32),
            shape((1, units // cols), f32),
            shape((units // cols, classes), f32),
            shape((1, classes), f32),
            shape((1, 1), f32),
        ],
        [pltpu.VMEM((2, height // 2, units), f32)],
        ids,
        grand,
        other,
        specs=[SMEM, VMEM, VMEM],
    )
    return (
        logits,
        mean_loss.reshape(()),
        grad_in,
        grad_bias_in.reshape(-1),
        grad_out,
        grad_bias_out.reshape(-1),
    )


def solution(mesh):
    in_specs = (
        P("col", "node"),
        P("node", None, None, None),
        P("node", None),
        P("node"),
        P("node"),
        P("node"),
        P("col", None),
        P("col"),
        P("col", None),
        P(),
    )
    out_specs = (P(None, "node"), P(), P("col", None), P("col"), P("col", None), P())
    return jax.shard_map(
        on_device, mesh=mesh, in_specs=in_specs, out_specs=out_specs, check_vma=False
    )
```

```python
import functools

import jax
import jax.numpy as jnp
from jax import lax
from jax.experimental import pallas as pl
from jax.experimental.pallas import tpu as pltpu
from jax.sharding import PartitionSpec as P

BLOCK = 128
CHUNK = 4
UNROLL = 8
DEPTH = 3
PAD = 48
HALF = 24

f32 = jnp.float32
bf16 = jnp.bfloat16
VMEM = pl.BlockSpec(memory_space=pltpu.VMEM)
SMEM = pl.BlockSpec(memory_space=pltpu.SMEM)
MIB = 1 << 20

CURVE = 0.7978845608028654
CUBIC = 0.044715


def exchange(value, axis, offset):
    total = lax.axis_size(axis)
    return lax.ppermute(value, axis, [(i, i ^ offset) for i in range(total)])


def split(value):
    high = value.astype(bf16)
    low = (value - high.astype(f32)).astype(bf16)
    return high, low


def product(left, right, dims):
    lh, ll = split(left)
    rh, rl = split(right)

    def one(a, b):
        return lax.dot_general(a, b, (dims, ((), ())), preferred_element_type=f32)

    return one(lh, rh) + (one(lh, rl) + one(ll, rh))


def call(body, outs, scratch, *args, specs=None, out_specs=None, limit=20, flops=0, moved=0):
    return pl.pallas_call(
        body,
        out_shape=outs,
        in_specs=specs or [VMEM] * len(args),
        out_specs=out_specs or [VMEM] * len(outs),
        scratch_shapes=scratch,
        compiler_params=pltpu.CompilerParams(vmem_limit_bytes=limit * MIB),
        cost_estimate=pl.CostEstimate(flops=flops, bytes_accessed=moved, transcendentals=0),
    )(*args)


def as_column(row):
    size = row.shape[1]
    shape = (size, size)
    same = lax.broadcasted_iota(jnp.int32, shape, 0) == lax.broadcasted_iota(jnp.int32, shape, 1)
    return jnp.sum(jnp.where(same, row, 0.0), axis=1, keepdims=True)


def as_row(column):
    size = column.shape[0]
    shape = (size, size)
    same = lax.broadcasted_iota(jnp.int32, shape, 0) == lax.broadcasted_iota(jnp.int32, shape, 1)
    return jnp.sum(jnp.where(same, column, 0.0), axis=0, keepdims=True)


def pack_body(
    count_in, column_in, tiles_ref, pack_ref, list_ref, row_ref, total_ref,
    count_ref, column_ref, land, place, owner, twin_from, twin_to, sem, list_sem,
):
    rows, slots = column_ref.shape
    lists = [
        pltpu.make_async_copy(count_in, count_ref, list_sem.at[0]),
        pltpu.make_async_copy(column_in, column_ref, list_sem.at[1]),
    ]
    for copy in lists:
        copy.start()
    for copy in lists:
        copy.wait()

    def copies(row, act):
        ring = lax.rem(row, DEPTH)
        live = count_ref[row]
        for power in range(slots.bit_length()):
            size = 1 << power

            @pl.when(live & size != 0)
            def _():
                first = live & ~(2 * size - 1)
                act(
                    pltpu.make_async_copy(
                        tiles_ref.at[row, pl.ds(first, size)],
                        land.at[pl.ds(ring * slots + first, size)],
                        sem.at[ring, power],
                    )
                )

    def start(copy):
        copy.start()

    def wait(copy):
        copy.wait()

    for row in range(DEPTH):
        copies(row, start)
    land[DEPTH * slots] = jnp.zeros((BLOCK, BLOCK), f32)

    def clear(index, _):
        place[index] = -1
        return 0

    lax.fori_loop(0, place.shape[0], clear, 0)

    def one_row(row, begin):
        stamp = row * slots
        shift = stamp - lax.rem(row, DEPTH) * slots

        def scan(slot, state):
            found, twins = state
            column = column_ref[row, slot]
            at = place[column]
            fresh = at < stamp
            place[column] = jnp.where(fresh, stamp + slot, at)
            owner[found] = stamp - shift + slot
            list_ref[begin * CHUNK + found] = column
            twin_from[twins] = stamp - shift + slot
            twin_to[twins] = at - shift
            step = fresh.astype(jnp.int32)
            return found + step, twins + 1 - step

        found, twins = lax.fori_loop(0, count_ref[row], scan, (0, 0))
        steps = (found + CHUNK - 1) // CHUNK

        def blank(index, _):
            list_ref[begin * CHUNK + index] = 0
            owner[index] = DEPTH * slots
            return 0

        lax.fori_loop(found, steps * CHUNK, blank, 0)
        copies(row, wait)

        def join(index, _):
            to = twin_to[index]
            land[to] = land[to] + land[twin_from[index]]
            return 0

        lax.fori_loop(0, twins, join, 0)

        def convert(step, _):
            item = begin + step
            row_ref[item] = row
            for q in range(CHUNK):
                at = slice(q * BLOCK, (q + 1) * BLOCK)
                high, low = split(land[owner[step * CHUNK + q]])
                pack_ref[item, :BLOCK, at] = high
                pack_ref[item, BLOCK:, at] = low
            return 0

        lax.fori_loop(0, steps, convert, 0)

        @pl.when(row + DEPTH < rows)
        def _():
            copies(row + DEPTH, start)

        return begin + steps

    used = lax.fori_loop(0, rows, one_row, 0)
    total = (used + UNROLL - 1) // UNROLL * UNROLL

    def fill(item, _):
        row_ref[item] = 0
        for q in range(CHUNK):
            list_ref[item * CHUNK + q] = 0
        pack_ref[item] = jnp.zeros(pack_ref.shape[1:], bf16)
        return 0

    lax.fori_loop(used, total, fill, 0)
    total_ref[0] = total // UNROLL


def pack(tiles, tile_column, tile_count, block_total):
    rows, slots = tile_column.shape
    items = -(-rows * slots // (CHUNK * UNROLL)) * UNROLL
    shape = jax.ShapeDtypeStruct
    return call(
        pack_body,
        [
            pltpu.VMEM((items, 2 * BLOCK, CHUNK * BLOCK), bf16),
            shape((items * CHUNK,), jnp.int32),
            shape((items,), jnp.int32),
            shape((1,), jnp.int32),
        ],
        [
            pltpu.SMEM(tile_count.shape, jnp.int32),
            pltpu.SMEM(tile_column.shape, jnp.int32),
            pltpu.VMEM((DEPTH * slots + 1, BLOCK, BLOCK), f32),
            pltpu.SMEM((block_total,), jnp.int32),
            pltpu.SMEM((slots,), jnp.int32),
            pltpu.SMEM((slots,), jnp.int32),
            pltpu.SMEM((slots,), jnp.int32),
            pltpu.SemaphoreType.DMA((DEPTH, slots.bit_length())),
            pltpu.SemaphoreType.DMA((2,)),
        ],
        pltpu.with_memory_space_constraint(tile_count, pltpu.HBM),
        pltpu.with_memory_space_constraint(tile_column, pltpu.HBM),
        tiles,
        specs=[pl.BlockSpec(memory_space=pl.ANY)] * 3,
        out_specs=[VMEM, SMEM, SMEM, SMEM],
        limit=20,
        flops=10**8,
        moved=40 * MIB,
    )


def bring(total_ref, pack_ref, store, sem):
    def one(group):
        part = pl.ds(group * UNROLL, UNROLL)
        return pltpu.make_async_copy(pack_ref.at[part], store.at[part], sem.at[group])

    def start(group, _):
        one(group).start()
        return 0

    lax.fori_loop(0, total_ref[0], start, 0)
    return one


def store_block(values, at, value):
    channels = value.shape[0]
    high, low = split(value)
    values[at, :channels] = high
    values[at, channels:] = low


def mix_rows(total_ref, list_ref, row_ref, store, values, sums):
    sums[...] = jnp.zeros_like(sums)

    def step(group, _):
        for part in range(UNROLL):
            item = group * UNROLL + part
            left = jnp.concatenate([values[list_ref[item * CHUNK + q]] for q in range(CHUNK)], axis=1)
            row = row_ref[item]
            sums[row] = sums[row] + lax.dot_general(
                left, store[item], (((1,), (1,)), ((), ())), preferred_element_type=f32
            )
        return 0

    lax.fori_loop(0, total_ref[0], step, 0)


def mixed_row(sums, row):
    total = sums[row]
    channels = total.shape[0] // 2
    total = total[:, :BLOCK] + total[:, BLOCK:]
    return total[:channels] + total[channels:]


def mix_in_body(nodes, cols, ids_ref, total_ref, list_ref, row_ref, pack_ref, *refs):
    pieces, outs = refs[:nodes], refs[nodes : nodes + cols]
    values, sums = refs[nodes + cols :]
    rows = sums.shape[0]
    node, col = ids_ref[0], ids_ref[1]
    for offset in range(nodes):
        base = (node ^ offset) * rows
        for part in range(rows):
            store_block(values, base + part, pieces[offset][:, part * BLOCK : (part + 1) * BLOCK])
    mix_rows(total_ref, list_ref, row_ref, pack_ref, values, sums)
    slice_rows = rows // cols
    for offset in range(cols):
        for part in range(slice_rows):
            row = (col ^ offset) * slice_rows + part
            outs[offset][:, part * BLOCK : (part + 1) * BLOCK] = mixed_row(sums, row)


def dense_body(cols, per, ids_ref, *refs):
    pieces, weights = refs[:cols], refs[cols : 2 * cols]
    mixed_ref, hidden_ref, slope_ref, weight_out_ref = refs[2 * cols + 1 : 2 * cols + 5]
    outs = refs[2 * cols + 5 : 3 * cols + 5]
    held, held_weights, scores = refs[-3:]
    col = ids_ref[1]
    for offset in range(cols):
        held[col ^ offset] = pieces[offset][...]
        held_weights[col ^ offset] = weights[offset][...]
    feats = held.shape[1]
    units, classes = weight_out_ref.shape
    mixed = held[...].reshape(mixed_ref.shape)
    mixed_ref[...] = mixed
    weight_in = held_weights[:, :feats].reshape(feats * cols, units)
    own = units // cols
    weight_out = held_weights[:, feats : feats + own].reshape(units, units)[:, :classes]
    weight_out_ref[...] = weight_out
    bias_in = jnp.concatenate(
        [held_weights[group, feats + own : feats + own + 1, :own] for group in range(cols)], axis=1
    )
    inner = product(weight_in, mixed, ((0,), (0,))) + as_column(bias_in)
    bend = jnp.tanh(CURVE * (inner + CUBIC * inner * inner * inner))
    hidden = 0.5 * inner * (1.0 + bend)
    hidden_ref[...] = hidden
    slope_ref[...] = 0.5 * (1.0 + bend) + (0.5 * inner) * (1.0 - bend * bend) * (
        CURVE * (1.0 + 3.0 * CUBIC * inner * inner)
    )
    value = product(weight_out, hidden, ((0,), (0,)))
    scores[...] = jnp.zeros_like(scores)
    for group in range(cols):
        scores[group, :per] = value[group * per : (group + 1) * per]
    for offset in range(cols):
        outs[offset][...] = scores[col ^ offset]


def stack_body(*refs):
    for index, ref in enumerate(refs[:-2]):
        refs[-1][index] = ref[...]


def mix_out_body(nodes, cols, per, ids_ref, total_ref, list_ref, row_ref, pack_ref, bias_ref, labels_ref, *refs):
    pieces = refs[:nodes]
    upper_ref, lower_ref, stats_ref, values, sums, groups = refs[nodes:]
    rows = sums.shape[0]
    node, col = ids_ref[0], ids_ref[1]
    slice_rows = rows // cols
    column = as_column(bias_ref[...])
    groups[...] = jnp.zeros_like(groups)
    for group in range(cols):
        groups[group, :per] = column[group * per : (group + 1) * per]
    for offset in range(nodes):
        base = (node ^ offset) * rows
        for group in range(cols):
            for part in range(slice_rows):
                store_block(
                    values,
                    base + (col ^ group) * slice_rows + part,
                    pieces[offset][group, :, part * BLOCK : (part + 1) * BLOCK],
                )
    mix_rows(total_ref, list_ref, row_ref, pack_ref, values, sums)
    for row in range(rows):
        at = slice(row * BLOCK, (row + 1) * BLOCK)
        total = mixed_row(sums, row) + groups[col]
        upper_ref[:, at] = total[:HALF]
        lower_ref[:, at] = total[HALF:]
    logits = jnp.concatenate([upper_ref[...], lower_ref[...]], axis=0)
    place = lax.broadcasted_iota(jnp.int32, logits.shape, 0)
    inside = place < per
    top = jnp.max(jnp.where(inside, logits, -jnp.inf), axis=0, keepdims=True)
    total = jnp.sum(jnp.where(inside, jnp.exp(logits - top), 0.0), axis=0, keepdims=True)
    hit = inside & (place + col * per == labels_ref[...])
    chosen = jnp.sum(jnp.where(hit, logits, 0.0), axis=0, keepdims=True)
    for kind, value in enumerate((top, total, chosen)):
        for row in range(rows):
            stats_ref[kind * rows + row : kind * rows + row + 1] = value[:, row * BLOCK : (row + 1) * BLOCK]


def mix_back_body(nodes, cols, per, ids_ref, total_ref, list_ref, row_ref, pack_ref, upper_ref, lower_ref, labels_ref, mask_ref, *refs):
    stats, outs = refs[:cols], refs[cols : cols + nodes]
    extra_ref, sums, grads = refs[cols + nodes :]
    rows = grads.shape[0]
    node, col = ids_ref[0], ids_ref[1]

    def unfold(kind, ref):
        lines = [ref[kind * rows + row : kind * rows + row + 1] for row in range(rows)]
        return jnp.concatenate(lines, axis=1)

    tops = [unfold(0, ref) for ref in stats]
    top = functools.reduce(jnp.maximum, tops)
    total = sum(unfold(1, ref) * jnp.exp(at - top) for ref, at in zip(stats, tops))
    chosen = sum(unfold(2, ref) for ref in stats)
    mask = mask_ref[...].astype(f32)
    logits = jnp.concatenate([upper_ref[...], lower_ref[...]], axis=0)
    place = lax.broadcasted_iota(jnp.int32, logits.shape, 0)
    inside = place < per
    hit = place + col * per == labels_ref[...]
    chance = jnp.exp(logits - top) * (1.0 / total)
    grad = jnp.where(inside, mask * (chance - hit.astype(f32)), 0.0)
    high, low = split(grad)
    ones = jnp.ones((8, grad.shape[1]), bf16)
    bias_row = lax.dot_general(
        ones, high, (((1,), (1,)), ((), ())), preferred_element_type=f32
    ) + lax.dot_general(ones, low, (((1,), (1,)), ((), ())), preferred_element_type=f32)
    loss = jnp.sum(mask * (top + jnp.log(total) - chosen), axis=1, keepdims=True)
    number = jnp.sum(mask, axis=1, keepdims=True)
    first = (col == 0).astype(f32)
    extra_ref[...] = jnp.zeros_like(extra_ref)
    line = lax.broadcasted_iota(jnp.int32, bias_row.shape, 0)
    extra_ref[:, : high.shape[0]] = jnp.where(line == col, bias_row, 0.0)
    extra_ref[cols : cols + 1, 0:1] = loss * first
    extra_ref[cols : cols + 1, 1:2] = number * first

    for row in range(rows):
        at = slice(row * BLOCK, (row + 1) * BLOCK)
        grads[row] = jnp.concatenate(
            [
                jnp.concatenate([high[:, at], high[:, at]], axis=1),
                jnp.concatenate([low[:, at], low[:, at]], axis=1),
            ],
            axis=0,
        )
    sums[...] = jnp.zeros_like(sums)

    def step(group, _):
        for part in range(UNROLL):
            item = group * UNROLL + part
            terms = jnp.dot(grads[row_ref[item]], pack_ref[item], preferred_element_type=f32)
            half = terms.shape[0] // 2
            terms = terms[:half] + terms[half:]
            for q in range(CHUNK):
                to = list_ref[item * CHUNK + q]
                sums[to] = sums[to] + terms[:, q * BLOCK : (q + 1) * BLOCK]
        return 0

    lax.fori_loop(0, total_ref[0], step, 0)
    for offset in range(nodes):
        base = (node ^ offset) * rows
        for part in range(rows):
            outs[offset][:, part * BLOCK : (part + 1) * BLOCK] = sums[base + part]


def pair_body(*refs):
    count = len(refs) // 3
    for index in range(count):
        refs[2 * count + index][...] = refs[index][...] + refs[count + index][...]


def sum_body(cols, ids_ref, *refs):
    parts, outs, held = refs[: -cols - 1], refs[-cols - 1 : -1], refs[-1]
    col = ids_ref[1]
    total = sum((ref[...] for ref in parts[1:]), parts[0][...])
    width = total.shape[1] // cols
    for group in range(cols):
        held[group] = total[:, group * width : (group + 1) * width]
    for offset in range(cols):
        outs[offset][...] = held[col ^ offset]


def grads_body(cols, per, ids_ref, mixed_ref, hidden_ref, slope_ref, weight_out_ref, extra_ref, *refs):
    pieces = refs[:cols]
    keep_ref, send_ref, held, packed = refs[cols:]
    core, col = ids_ref[0] & 1, ids_ref[1]
    for offset in range(cols):
        held[col ^ offset] = pieces[offset][...]
    spread = jnp.concatenate([held[group, :per] for group in range(cols)], axis=0)
    hidden_grad = product(weight_out_ref[...], spread, ((1,), (0,)))
    inner_grad = hidden_grad * slope_ref[...]
    weight_in = product(mixed_ref[...], inner_grad, ((1,), (1,)))
    weight_out = product(spread, hidden_ref[...], ((1,), (1,)))
    bias_in = as_row(jnp.sum(inner_grad, axis=1, keepdims=True))
    feats, units = weight_in.shape[0] // cols, weight_out.shape[1] // cols
    extra = extra_ref[: cols + 1]
    line = lax.broadcasted_iota(jnp.int32, extra.shape, 0)
    for group in range(cols):
        mine = slice(group * units, (group + 1) * units)
        folded = jnp.concatenate([weight_out[q * per : (q + 1) * per, mine] for q in range(cols)], axis=1)
        spare = jnp.zeros((1, BLOCK), f32)
        bias = jnp.concatenate([spare, bias_in[:, mine], spare[:, : BLOCK - units]], axis=1)
        packed[group] = jnp.concatenate(
            [weight_in[group * feats : (group + 1) * feats], folded, jnp.where(line == cols, extra + bias, extra)],
            axis=0,
        )
    half = packed.shape[1] // 2
    for offset in range(cols):
        keep_ref[offset] = packed[col ^ offset, pl.ds(pl.multiple_of(core * half, 8), half)]
        send_ref[offset] = packed[col ^ offset, pl.ds(pl.multiple_of((1 - core) * half, 8), half)]


def finish_body(cols, per, ids_ref, mine_ref, other_ref, weight_in_ref, bias_in_ref, weight_out_ref, bias_out_ref, loss_ref, whole):
    core = ids_ref[0] & 1
    half = mine_ref.shape[0]
    whole[core] = mine_ref[...]
    whole[1 - core] = other_ref[...]
    value = whole[...].reshape(2 * half, mine_ref.shape[1])
    feats, (units, classes) = weight_in_ref.shape[0], weight_out_ref.shape
    weight_in_ref[...] = value[:feats]
    folded = value[feats : feats + per]
    spread = jnp.concatenate([folded[:, q * units : (q + 1) * units] for q in range(cols)], axis=0)
    weight_out_ref[...] = spread.T
    extra = value[feats + per : feats + per + cols + 1]
    bias_in_ref[...] = extra[cols : cols + 1, BLOCK : BLOCK + units]
    bias_out_ref[...] = jnp.concatenate([extra[group : group + 1, :per] for group in range(cols)], axis=1)
    loss_ref[...] = extra[cols : cols + 1, 0:1] / jnp.maximum(extra[cols : cols + 1, 1:2], 1.0)


def logits_body(cols, per, ids_ref, *refs):
    uppers, lowers, out_ref, held = refs[:cols], refs[cols : 2 * cols], refs[-2], refs[-1]
    col = ids_ref[1]
    for offset in range(cols):
        held[col ^ offset, :HALF] = uppers[offset][...]
        held[col ^ offset, HALF:] = lowers[offset][...]
    out_ref[...] = jnp.concatenate([held[group, :per] for group in range(cols)], axis=0)


def gather_chips(value, nodes):
    return [value] + [exchange(value, "node", offset) for offset in range(2, nodes, 2)]


def gather_cores(even):
    odd = [exchange(piece, "node", 1) for piece in even]
    return [piece for pair in zip(even, odd) for piece in pair]


def on_device(
    features,
    tiles,
    tile_column,
    tile_count,
    labels,
    train_mask,
    weight_in,
    bias_in,
    weight_out,
    bias_out,
):
    nodes, cols = lax.axis_size("node"), lax.axis_size("col")
    rows = tile_column.shape[0]
    local = labels.shape[0]
    slice_nodes = local // cols
    block_total = nodes * rows
    feats = features.shape[0]
    classes = weight_out.shape[1]
    per = classes // cols
    units = weight_out.shape[0] * cols
    shape = jax.ShapeDtypeStruct
    ids = jnp.stack([lax.axis_index("node"), lax.axis_index("col")]).astype(jnp.int32)

    labels = labels[None, :]
    train_mask = train_mask[None, :]
    own = units // cols
    height = feats + own + 8
    weights = (
        jnp.pad(weight_in, ((0, height - feats), (0, 0)))
        + jnp.pad(weight_out, ((feats, 8), (0, units - classes)))
        + jnp.pad(bias_in[None, :], ((feats + own, 7), (0, units - own)))
    )
    ids, tile_count = lax.optimization_barrier((ids, tile_count))
    even = gather_chips(features, nodes)
    weight_pieces = [weights] + [exchange(weights, "col", k) for k in range(1, cols)]
    packed, listed, placed, steps = pack(tiles, tile_column, tile_count, block_total)
    steps, even, weight_pieces = lax.optimization_barrier((steps, even, weight_pieces))
    feature_pieces = gather_cores(even)
    packed = pltpu.with_memory_space_constraint(packed, pltpu.VMEM)
    sparse = (ids, steps, listed, placed, packed)
    sparse_specs = [SMEM] * 4 + [VMEM]

    mixed_parts = call(
        functools.partial(mix_in_body, nodes, cols),
        [shape((feats, slice_nodes), f32)] * cols,
        [pltpu.VMEM((block_total, 2 * feats, BLOCK), bf16), pltpu.VMEM((rows, 2 * feats, 2 * BLOCK), f32)],
        *sparse,
        *feature_pieces,
        specs=sparse_specs + [VMEM] * nodes,
        limit=20,
        flops=10**9,
        moved=16 * MIB,
    )
    mixed_pieces = [mixed_parts[0]] + [exchange(mixed_parts[k], "col", k) for k in range(1, cols)]
    mixed, hidden, slope, weight_out_all, *score_parts = call(
        functools.partial(dense_body, cols, per),
        [shape((feats * cols, slice_nodes), f32)]
        + [shape((units, slice_nodes), f32)] * 2
        + [shape((units, classes), f32)]
        + [shape((PAD, slice_nodes), f32)] * cols,
        [
            pltpu.VMEM((cols, feats, slice_nodes), f32),
            pltpu.VMEM((cols, *weights.shape), f32),
            pltpu.VMEM((cols, PAD, slice_nodes), f32),
        ],
        ids,
        *mixed_pieces,
        *weight_pieces,
        packed,
        specs=[SMEM] + [VMEM] * (2 * cols + 1),
        flops=10**8,
        moved=2 * MIB,
    )
    score_pieces = [score_parts[0]] + [exchange(score_parts[k], "col", k) for k in range(1, cols)]
    (stacked,) = call(
        stack_body,
        [shape((cols, PAD, slice_nodes), f32)],
        [],
        *score_pieces, packed,
        limit=20,
        moved=MIB,
    )
    scores = gather_cores(gather_chips(stacked, nodes))
    upper, lower, stats = call(
        functools.partial(mix_out_body, nodes, cols, per),
        [shape((HALF, local), f32), shape((PAD - HALF, local), f32), shape((3 * rows, BLOCK), f32)],
        [pltpu.VMEM((block_total, 2 * PAD, BLOCK), bf16), pltpu.VMEM((rows, 2 * PAD, 2 * BLOCK), f32), pltpu.VMEM((cols, PAD, 1), f32)],
        *sparse,
        bias_out[None, :],
        labels,
        *scores,
        specs=sparse_specs + [VMEM] * (2 + nodes),
        limit=20,
        flops=10**9,
        moved=16 * MIB,
    )
    stats_pieces = [stats] + [exchange(stats, "col", k) for k in range(1, cols)]
    *spread_parts, extra = call(
        functools.partial(mix_back_body, nodes, cols, per),
        [shape((PAD, local), f32)] * nodes + [shape((8, 2 * BLOCK), f32)],
        [
            pltpu.VMEM((block_total, PAD, BLOCK), f32),
            pltpu.VMEM((rows, 2 * PAD, 2 * BLOCK), bf16),
        ],
        *sparse,
        upper,
        lower,
        labels,
        train_mask,
        *stats_pieces,
        specs=sparse_specs + [VMEM] * (4 + cols),
        limit=20,
        flops=10**9,
        moved=16 * MIB,
    )
    uppers = [upper] + [exchange(upper, "col", k) for k in range(1, cols)]
    spread_parts, uppers = lax.optimization_barrier((spread_parts, uppers))
    paired = call(
        pair_body,
        [shape((PAD, local), f32)] * (nodes // 2),
        [],
        *spread_parts[::2],
        *[exchange(part, "node", 1) for part in spread_parts[1::2]],
        limit=20,
        moved=2 * MIB,
    )
    paired, lower = lax.optimization_barrier((paired, lower))
    chips = [exchange(paired[k], "node", 2 * k) for k in range(1, nodes // 2)]
    lowers = [lower] + [exchange(lower, "col", k) for k in range(1, cols)]
    spread_slices = call(
        functools.partial(sum_body, cols),
        [shape((PAD, slice_nodes), f32)] * cols,
        [pltpu.VMEM((cols, PAD, slice_nodes), f32)],
        ids,
        paired[0],
        *chips,
        specs=[SMEM] + [VMEM] * (nodes // 2),
        limit=20,
        moved=MIB,
    )
    spread_pieces = [spread_slices[0]] + [exchange(spread_slices[k], "col", k) for k in range(1, cols)]
    (logits,) = call(
        functools.partial(logits_body, cols, per),
        [shape((classes, local), f32)],
        [pltpu.VMEM((cols, PAD, local), f32)],
        ids,
        *uppers,
        *lowers,
        specs=[SMEM] + [VMEM] * (2 * cols),
        limit=20,
        moved=2 * MIB,
    )
    logits, *spread_pieces = lax.optimization_barrier((logits, *spread_pieces))

    height = feats + per + cols + 1
    keep, send = call(
        functools.partial(grads_body, cols, per),
        [shape((cols, height // 2, units), f32)] * 2,
        [pltpu.VMEM((cols, PAD, slice_nodes), f32), pltpu.VMEM((cols, height, units), f32)],
        ids,
        mixed,
        hidden,
        slope,
        weight_out_all,
        extra,
        *spread_pieces,
        specs=[SMEM] + [VMEM] * (5 + cols),
        flops=10**8,
        moved=2 * MIB,
    )
    halves = keep + exchange(send, "node", 1)
    total = halves[0]
    for k in range(1, cols):
        total = total + exchange(halves[k], "col", k)
    grand = total
    for k in range(2, nodes, 2):
        grand = grand + exchange(total, "node", k)
    other = exchange(grand, "node", 1)
    grad_in, grad_bias_in, grad_out, grad_bias_out, mean_loss = call(
        functools.partial(finish_body, cols, per),
        [
            shape((feats, units), f32),
            shape((1, units // cols), f32),
            shape((units // cols, classes), f32),
            shape((1, classes), f32),
            shape((1, 1), f32),
        ],
        [pltpu.VMEM((2, height // 2, units), f32)],
        ids,
        grand,
        other,
        specs=[SMEM, VMEM, VMEM],
    )
    return (
        logits,
        mean_loss.reshape(()),
        grad_in,
        grad_bias_in.reshape(-1),
        grad_out,
        grad_bias_out.reshape(-1),
    )


def solution(mesh):
    in_specs = (
        P("col", "node"),
        P("node", None, None, None),
        P("node", None),
        P("node"),
        P("node"),
        P("node"),
        P("col", None),
        P("col"),
        P("col", None),
        P(),
    )
    out_specs = (P(None, "node"), P(), P("col", None), P("col"), P("col", None), P())
    return jax.shard_map(
        on_device, mesh=mesh, in_specs=in_specs, out_specs=out_specs, check_vma=False
    )
```
